128 devices in a mesh: tx: 8 (over y, core), ty: 16 (over z, x).
Axes of the slice: x: 4, y: 4, z: 4, core: 2. Of those that a mesh axis runs over, the one named last changes fastest.
Arguments:
- probes: bfloat16 [512, 64, 2048], P(('tx', 'ty')), may hold values from -6 to 6
- points: float32 [512, 8, 2048], P(('tx', 'ty')), may hold values from 0 to 1
- up_basis: bfloat16 [512, 256, 2048], P(('tx', 'ty')), may hold values from -0.125 to 0.125
- down_basis: bfloat16 [512, 256, 2048], P(('tx', 'ty')), may hold values from -0.09375 to 0.09375
- box_skeleton: int32 [512, 256], P(('tx', 'ty')), may hold values from 0 to 2047, as said below
- box_transfer: bfloat16 [512, 256, 256], P(('tx', 'ty')), may hold values from -0.375 to 0.375
- node_skeleton: int32 [128, 256], P(('tx', 'ty')), may hold values from 0 to 1023, as said below
- node_transfer: bfloat16 [128, 256, 256], P(('tx', 'ty')), may hold values from -0.375 to 0.375
- group_skeleton: int32 [8, 256], replicated, may hold values from 0 to 4095, as said below
- near_list: int32 [512, 3], P(('tx', 'ty')), may hold values from -1 to 511, as said below
- node_list: int32 [128, 8], P(('tx', 'ty')), may hold values from 0 to 127, as said below
Outputs:
- applied: bfloat16 [512, 64, 2048], P(('tx', 'ty'))
The draws below stay inside these ranges and needn't reach their ends.
Inputs may be any that keep to these rules, and one draw needn't show every extreme that they name: `box_skeleton`: each row names 256 distinct points of its box. `node_skeleton`: each row names 256 distinct points among the 1024 skeleton points of the node's boxes, numbered box by box. `group_skeleton`: each row names 256 distinct points among the 4096 skeleton points of the group's middle-level nodes, numbered node by node. `near_list`: box b of node d names 1 to 3 distinct boxes, live entries first and -1 after them; every named box belongs to d or to the nodes d - 1 and d + 1 where these lie in d's upper-level node. `node_list`: node d names 8 distinct nodes of its own upper-level node whose ty index differs from d's by two or more.
All inputs are finite; a program needn't handle non-finite values.
Results may differ from the reference program's by a relative error of at most 0.024.
Values may be sent and summed in bfloat16 or wider, within the bound.
No kernel may reach another device: no remote copies, remote signals or barrier semaphores. Data moves between devices by JAX's collectives and lax.ppermute only.
A program may use at most 128 MiB of HBM per device.

```python
import jax
import jax.numpy as jnp
from jax import lax

BOXES = 4
LEAF = 2048
RANK = 256
PROBES = 64
FEAT = 8
NEAR = 3
NODES = 128
NBOX = 512
NODE_LIST = 8
N_TX = 8
N_TY = 16


def distinct_rows(key, rows, pool, count):
    bits = jax.random.randint(key, (rows, pool), 0, 2 ** 30 // pool)
    scores = bits * pool + jnp.arange(pool, dtype=jnp.int32)[None, :]
    return jnp.argsort(scores, axis=1)[:, :count].astype(jnp.int32)


def draw_box_skeleton(key, part):
    key = jax.random.fold_in(key, 1)
    return distinct_rows(key, BOXES * N_TX * N_TY, LEAF, RANK)


def draw_node_skeleton(key, part):
    key = jax.random.fold_in(key, 2)
    return distinct_rows(key, N_TX * N_TY, BOXES * RANK, RANK)


def draw_group_skeleton(key, part):
    key = jax.random.fold_in(key, 3)
    return distinct_rows(key, N_TX, N_TY * RANK, RANK)


def draw_near_list(key, part):
    key = jax.random.fold_in(key, 4)
    first_key, second_key = jax.random.split(key)
    total_boxes = BOXES * N_TX * N_TY
    box_ids = jnp.arange(total_boxes, dtype=jnp.int32)
    owner = box_ids // BOXES
    row_pos = owner % N_TY
    slots = jnp.arange(3 * BOXES, dtype=jnp.int32)
    candidate = owner[:, None] * BOXES - BOXES + slots[None, :]
    invalid = (slots[None, :] < BOXES) & (row_pos[:, None] == 0) | (slots[None, :] >= 2 * BOXES) & (row_pos[:, None] == N_TY - 1)
    bits = jax.random.randint(first_key, (total_boxes, 3 * BOXES), 0, 2 ** 20)
    scores = bits * 64 + slots[None, :] + jnp.where(invalid, 2 ** 28, 0)
    order = jnp.argsort(scores, axis=1)[:, :NEAR]
    picked = jnp.take_along_axis(candidate, order, axis=1)
    live = jax.random.randint(second_key, (total_boxes, 1), 1, NEAR + 1)
    return jnp.where(jnp.arange(NEAR, dtype=jnp.int32)[None, :] < live, picked, -1).astype(jnp.int32)


def draw_node_list(key, part):
    key = jax.random.fold_in(key, 5)
    total_nodes = N_TX * N_TY
    node_ids = jnp.arange(total_nodes, dtype=jnp.int32)
    row_pos = node_ids % N_TY
    group_ids = node_ids // N_TY
    columns = jnp.arange(N_TY, dtype=jnp.int32)
    invalid = jnp.abs(columns[None, :] - row_pos[:, None]) <= 1
    bits = jax.random.randint(key, (total_nodes, N_TY), 0, 2 ** 20)
    scores = bits * 64 + columns[None, :] + jnp.where(invalid, 2 ** 28, 0)
    order = jnp.argsort(scores, axis=1)[:, :NODE_LIST].astype(jnp.int32)
    return (group_ids[:, None] * N_TY + order).astype(jnp.int32)


def steps_of(key, shape, cuts, smallest, top_value):
    gain = 1.0
    for axis_at, blocks in cuts:
        draws = jax.random.uniform(jax.random.fold_in(jax.random.fold_in(key, 6), axis_at), (blocks,), jnp.float32, smallest / len(cuts), top_value / len(cuts))
        gain = gain * jnp.repeat(jnp.exp(draws), shape[axis_at] // blocks).reshape((-1,) + (1,) * (len(shape) - 1 - axis_at))
    return gain


def gaussian(own_key, shape, width, most, pieces=(), kind=jnp.bfloat16):
    factor_of = steps_of(own_key, shape, pieces, -0.22, 0.18) if pieces else 1.0
    drawn = jax.random.normal(own_key, shape, jnp.float32) * width * factor_of
    return jnp.minimum(jnp.maximum(drawn, -most), most).astype(kind)


def setup_inputs(seed: int = 0) -> dict:
    arg_keys = jax.random.split(jax.random.key(seed), 12)
    return {
        "probes": gaussian(arg_keys[0], (NBOX, PROBES, LEAF), 1.0, 6.0, ((0, 128),)),
        "points": jnp.clip(1.0 * jax.random.uniform(arg_keys[1], (NBOX, FEAT, LEAF), jnp.float32) ** steps_of(arg_keys[1], (NBOX, FEAT, LEAF), ((0, 128),), -0.2, 0.2), 0.0, 1.0),
        "up_basis": gaussian(arg_keys[2], (NBOX, RANK, LEAF), LEAF ** -0.5, 0.125, ((0, 128),)),
        "down_basis": gaussian(arg_keys[3], (NBOX, RANK, LEAF), (16 * RANK) ** -0.5, 0.09375, ((0, 128),)),
        "box_skeleton": draw_box_skeleton(jax.random.fold_in(arg_keys[11], 71), 0),
        "box_transfer": gaussian(arg_keys[5], (NBOX, RANK, RANK), RANK ** -0.5, 0.375, ((0, 128),)),
        "node_skeleton": draw_node_skeleton(jax.random.fold_in(arg_keys[11], 71), 0),
        "node_transfer": gaussian(arg_keys[7], (NODES, RANK, RANK), RANK ** -0.5, 0.375, ((0, 128),)),
        "group_skeleton": draw_group_skeleton(jax.random.fold_in(arg_keys[11], 71), 0),
        "near_list": draw_near_list(jax.random.fold_in(arg_keys[11], 71), 0),
        "node_list": draw_node_list(jax.random.fold_in(arg_keys[11], 71), 0),
    }


inv_length = 4.0

def kernel_block(source, target):
    squared = jnp.zeros((source.shape[1], target.shape[1]), jnp.float32)
    for feature in range(source.shape[0]):
        offset = source[feature][:, None] - target[feature][None, :]
        squared = squared + offset * offset
    scaled = jnp.sqrt(squared) * inv_length
    return (scaled * jnp.exp(-scaled)).astype(jnp.bfloat16)

def reference(probes, points, up_basis, down_basis, box_skeleton, box_transfer, node_skeleton, node_transfer, group_skeleton, near_list, node_list):
    nodes = N_TX * N_TY
    highest = lax.Precision.HIGHEST

    def up_one(pair):
        return jnp.dot(pair[0], pair[1].T, preferred_element_type=jnp.float32).astype(jnp.bfloat16)
    box_weights = lax.map(up_one, (probes, up_basis))
    grouped = box_weights.reshape(nodes, BOXES, PROBES, RANK).astype(jnp.float32)
    transfers = box_transfer.reshape(nodes, BOXES, RANK, RANK).astype(jnp.float32)
    node_weights = jnp.einsum('dbqr,dbrs->dqs', grouped, transfers, precision=highest).astype(jnp.bfloat16)
    index_box = jnp.broadcast_to(box_skeleton[:, None, :], (NBOX, FEAT, RANK))
    box_points = jnp.take_along_axis(points, index_box, axis=2)
    pooled = jnp.transpose(box_points.reshape(nodes, BOXES, FEAT, RANK), (0, 2, 1, 3)).reshape(nodes, FEAT, BOXES * RANK)
    index_node = jnp.broadcast_to(node_skeleton[:, None, :], (nodes, FEAT, RANK))
    node_points = jnp.take_along_axis(pooled, index_node, axis=2)
    pooled_group = jnp.transpose(node_points.reshape(N_TX, N_TY, FEAT, RANK), (0, 2, 1, 3)).reshape(N_TX, FEAT, N_TY * RANK)
    index_group = jnp.broadcast_to(group_skeleton[:, None, :], (N_TX, FEAT, RANK))
    group_points = jnp.take_along_axis(pooled_group, index_group, axis=2)
    node_terms = jnp.einsum('dqr,drs->dqs', node_weights.astype(jnp.float32), node_transfer.astype(jnp.float32), precision=highest)
    group_weights = node_terms.reshape(N_TX, N_TY, PROBES, RANK).sum(axis=1).astype(jnp.bfloat16)

    def group_one(group_index):
        target = group_points[group_index]
        blocks = jax.vmap(kernel_block, in_axes=(0, None))(group_points, target)
        terms = jnp.einsum('gqr,grs->gqs', group_weights.astype(jnp.float32), blocks.astype(jnp.float32), precision=highest)
        keep = (jnp.arange(N_TX) != group_index)[:, None, None]
        return lax.optimization_barrier(jnp.sum(jnp.where(keep, terms, 0.0), axis=0)).astype(jnp.bfloat16)
    group_potential = lax.map(group_one, jnp.arange(N_TX, dtype=jnp.int32))

    def node_one(pair):
        node_index, entries = pair
        target = node_points[node_index]
        total = jnp.dot(group_potential[node_index // N_TY], node_transfer[node_index].T, preferred_element_type=jnp.float32)
        for entry in range(NODE_LIST):
            other = entries[entry]
            total = total + jnp.dot(node_weights[other], kernel_block(node_points[other], target), preferred_element_type=jnp.float32)
        return total.astype(jnp.bfloat16)
    node_potential = lax.map(node_one, (jnp.arange(nodes, dtype=jnp.int32), node_list))
    spread = jnp.repeat(node_potential, BOXES, axis=0).astype(jnp.float32)
    box_potential = jnp.einsum('bqs,brs->bqr', spread, box_transfer.astype(jnp.float32), precision=highest).astype(jnp.bfloat16)

    def leaf_one(group):
        entries, own_points, basis, potential = group
        total = jnp.dot(potential, basis, preferred_element_type=jnp.float32)
        for entry in range(NEAR):
            named = entries[entry]
            safe = jnp.maximum(named, 0)
            term = jnp.dot(probes[safe], kernel_block(points[safe], own_points), preferred_element_type=jnp.float32)
            total = total + jnp.where(named >= 0, term, 0.0)
        return total.astype(jnp.bfloat16)
    return lax.map(leaf_one, (near_list, points, down_basis, box_potential))
```

```python
import functools
import math

import jax
import jax.numpy as jnp
from jax import lax
from jax.experimental import pallas as pl
from jax.experimental.pallas import tpu as pltpu
from jax.sharding import PartitionSpec as P

bf16 = jnp.bfloat16
f32 = jnp.float32
i32 = jnp.int32

INV_LENGTH = 4.0
LN2 = math.log(2.0)
SCALE = INV_LENGTH / LN2
VMEM = pl.BlockSpec(memory_space=pltpu.VMEM)
SMEM = pl.BlockSpec(memory_space=pltpu.SMEM)
TILE_ROWS = 512
TILE_COLS = 1024
FIRST_UNITS = 2
SECOND_UNITS = 5
SLOTS = 12


def params(mib=48):
    return pltpu.CompilerParams(vmem_limit_bytes=mib * 2**20)


def split_points(points):
    scaled = (points - 0.5) * SCALE
    high = scaled.astype(bf16)
    low = (scaled - high.astype(f32)).astype(bf16)
    return high, low


def norm_rows(pair, one_first):
    high = pair[:8]
    low = pair[8:]
    full = high + low
    norm = jnp.sum(full * full, axis=0, keepdims=True)
    first = norm.astype(bf16).astype(f32)
    rest = norm - first
    second = rest.astype(bf16).astype(f32)
    third = rest - second
    row = lax.broadcasted_iota(i32, high.shape, 0)
    base = 3 if one_first else 0
    ones = 0 if one_first else 3
    out = jnp.where((row >= ones) & (row < ones + 3), 1.0, 0.0)
    out = jnp.where(row == base, first, out)
    out = jnp.where(row == base + 1, second, out)
    return jnp.where(row == base + 2, third, out)


def source_features(pair):
    high = pair[:8] * -2.0
    low = pair[8:] * -2.0
    return jnp.concatenate([high, low, high, norm_rows(pair, False)], axis=0).T.astype(bf16)


def target_features(pair):
    high = pair[:8]
    return jnp.concatenate([high, high, pair[8:], norm_rows(pair, True)], axis=0).astype(bf16)


def entries(squared):
    squared = jnp.maximum(squared, 1e-12)
    scaled = squared * lax.rsqrt(squared)
    return (scaled * jnp.exp2(-scaled)).astype(bf16)


def dot(a, b):
    return jnp.dot(a, b, preferred_element_type=f32)


def dot_nt(a, b):
    return lax.dot_general(a, b, (((1,), (1,)), ((), ())), preferred_element_type=f32)


def pack_kernel(near_ref, base_ref, probes_ref, points_ref, out_ref, table_ref):
    b = pl.program_id(0)
    out_ref[0, :64, :] = probes_ref[0]
    high, low = split_points(points_ref[0])
    out_ref[0, 64:80, :] = jnp.concatenate([high.astype(f32), low.astype(f32)], axis=0).astype(bf16)

    @pl.when(b == 0)
    def _():
        boxes, width = near_ref.shape
        count = i32(0)
        last = [i32(0), i32(0), i32(0)]
        own_count = i32(0)
        for own in (True, False):
            for box in range(boxes):
                for entry in range(width):
                    named = near_ref[box, entry]
                    slot = jnp.clip(named - base_ref[0], 0, 3 * boxes - 1)
                    side = (slot >= boxes).astype(i32) + (slot >= 2 * boxes).astype(i32)
                    mine = side == 1
                    take = (named >= 0) & (mine if own else jnp.logical_not(mine))
                    last = [jnp.where(take & (side == k), slot - k * boxes, last[k]) for k in range(3)]

                    @pl.when(take)
                    def _(count=count, box=box, side=side, last=tuple(last)):
                        table_ref[0, count] = side
                        table_ref[1, count] = i32(box)
                        table_ref[2, count] = last[0]
                        table_ref[3, count] = last[1]
                        table_ref[4, count] = last[2]

                    count = count + take.astype(i32)
            if own:
                own_count = count
        table_ref[5, 0] = count
        table_ref[5, 1] = own_count


def pack(near_list, base, probes, points):
    boxes, count, leaf = probes.shape
    return pl.pallas_call(
        pack_kernel,
        grid=(boxes,),
        in_specs=[
            SMEM,
            SMEM,
            pl.BlockSpec((1, count, leaf), lambda b: (b, 0, 0)),
            pl.BlockSpec((1, 8, leaf), lambda b: (b, 0, 0)),
        ],
        out_specs=[pl.BlockSpec((1, count + 16, leaf), lambda b: (b, 0, 0)), SMEM],
        out_shape=[
            jax.ShapeDtypeStruct((boxes, count + 16, leaf), bf16),
            jax.ShapeDtypeStruct((6, SLOTS), i32),
        ],
        compiler_params=params(),
        name="pack",
    )(near_list, base, probes, points)


def one_hot(index_row, size, offset=0):
    rows = lax.broadcasted_iota(i32, (size, index_row.shape[1]), 0) + offset
    return jnp.where(rows == index_row, 1.0, 0.0).astype(bf16)


def up_kernel(packed_ref, up_ref, box_skel_ref, transfer_ref, node_skel_ref, node_transfer_ref, out_ref, acc, pool):
    b = pl.program_id(0)
    boxes = pl.num_programs(0)
    rank = up_ref.shape[1]
    leaf = up_ref.shape[2]

    @pl.when(b == 0)
    def _():
        acc[...] = jnp.zeros_like(acc)

    weights = dot_nt(packed_ref[0, :64, :], up_ref[0]).astype(bf16)
    acc[...] += dot(weights, transfer_ref[0])
    pool[b] = dot(packed_ref[0, 64:80, :], one_hot(box_skel_ref[0], leaf)).astype(bf16)

    @pl.when(b == boxes - 1)
    def _():
        node_weight = acc[...].astype(bf16)
        out_ref[0:64, :] = node_weight
        found = jnp.zeros((16, rank), f32)
        for k in range(pool.shape[0]):
            found = found + dot(pool[k], one_hot(node_skel_ref[...], rank, k * rank))
        out_ref[64:80, :] = found.astype(bf16)
        out_ref[80:144, :] = dot(node_weight, node_transfer_ref[0]).astype(bf16)


def up_pass(packed, up_basis, box_skeleton, box_transfer, node_skeleton, node_transfer):
    boxes, rows, leaf = packed.shape
    rank = up_basis.shape[1]
    return pl.pallas_call(
        up_kernel,
        grid=(boxes,),
        in_specs=[
            pl.BlockSpec((1, rows, leaf), lambda b: (b, 0, 0)),
            pl.BlockSpec((1, rank, leaf), lambda b: (b, 0, 0)),
            pl.BlockSpec((1, 1, rank), lambda b: (b, 0, 0)),
            pl.BlockSpec((1, rank, rank), lambda b: (b, 0, 0)),
            pl.BlockSpec((1, rank), lambda b: (0, 0)),
            pl.BlockSpec((1, rank, rank), lambda b: (0, 0, 0)),
        ],
        out_specs=pl.BlockSpec((144, rank), lambda b: (0, 0)),
        out_shape=jax.ShapeDtypeStruct((144, rank), bf16),
        scratch_shapes=[pltpu.VMEM((64, rank), f32), pltpu.VMEM((boxes, 16, rank), bf16)],
        compiler_params=params(),
        name="up_pass",
    )(packed, up_basis, box_skeleton[:, None, :], box_transfer, node_skeleton, node_transfer)


def near_body(bounds, table, sources, target_ref, acc_ref, held, left, right):
    i = pl.program_id(0) + bounds[0]

    @pl.when(i < bounds[1])
    def _():
        side = table[0, i]
        box = table[1, i]
        for k, ref in sources:

            @pl.when(side == k)
            def _(ref=ref):
                held[...] = ref[0, :64, :]
                left[...] = source_features(ref[0, 64:80, :].astype(f32))

        right[...] = target_features(target_ref[0].astype(f32))
        leaf = left.shape[0]

        def columns(j, carry):
            cols = pl.ds(pl.multiple_of(j * TILE_COLS, TILE_COLS), TILE_COLS)
            total = acc_ref[box, :, cols]
            for k in range(leaf // TILE_ROWS):
                rows = slice(k * TILE_ROWS, (k + 1) * TILE_ROWS)
                block = entries(dot(left[rows, :], right[:, cols]))
                total = total + dot(held[:, rows], block)
            acc_ref[box, :, cols] = total
            return carry

        lax.fori_loop(0, leaf // TILE_COLS, columns, 0)


def near_first_kernel(bounds, table, own_ref, target_ref, acc_ref, held, left, right):
    @pl.when(pl.program_id(0) == 0)
    def _():
        acc_ref[...] = jnp.zeros_like(acc_ref)

    near_body(bounds, table, [(1, own_ref)], target_ref, acc_ref, held, left, right)


def near_kernel(bounds, table, own_ref, target_ref, prev_ref, next_ref, in_ref, acc_ref, held, left, right):
    @pl.when(pl.program_id(0) == 0)
    def _():
        acc_ref[...] = in_ref[...]

    near_body(bounds, table, [(0, prev_ref), (1, own_ref), (2, next_ref)], target_ref, acc_ref, held, left, right)


def last_unit(i, bounds):
    return jnp.maximum(jnp.minimum(i + bounds[0], bounds[1] - 1), 0)


def near_part(steps, bounds, table, packed, halo=None, acc=None):
    boxes, rows, leaf = packed.shape

    def source(row):
        def index(i, bounds, table):
            return (table[row, last_unit(i, bounds)], 0, 0)

        return pl.BlockSpec((1, rows, leaf), index)

    def target(i, bounds, table):
        return (table[1, last_unit(i, bounds)], 4, 0)

    in_specs = [source(3), pl.BlockSpec((1, 16, leaf), target)]
    args = [packed, packed]
    if halo is not None:
        in_specs += [source(2), source(4), pl.BlockSpec((boxes, 64, leaf), lambda i, bounds, table: (0, 0, 0))]
        args += [halo[0], halo[1], acc]
    tile = leaf * leaf
    return pl.pallas_call(
        near_first_kernel if halo is None else near_kernel,
        grid_spec=pltpu.PrefetchScalarGridSpec(
            num_scalar_prefetch=2,
            grid=(steps,),
            in_specs=in_specs,
            out_specs=pl.BlockSpec((boxes, 64, leaf), lambda i, bounds, table: (0, 0, 0)),
            scratch_shapes=[
                pltpu.VMEM((64, leaf), bf16),
                pltpu.VMEM((leaf, 32), bf16),
                pltpu.VMEM((32, leaf), bf16),
            ],
        ),
        out_shape=jax.ShapeDtypeStruct((boxes, 64, leaf), f32),
        compiler_params=params(),
        cost_estimate=pl.CostEstimate(
            flops=3 * 2 * tile * 320, bytes_accessed=8 * 2**20, transcendentals=3 * 2 * tile
        ),
        name="near_part",
    )(bounds, table, *args)


def fold_kernel(*refs):
    out_ref = refs[-1]
    total = jnp.zeros((64, out_ref.shape[1]), f32)
    for k, ref in enumerate(refs[:-1]):
        out_ref[k * 80 : (k + 1) * 80, :] = ref[0:80, :]
        total = total + ref[80:144, :].astype(f32)
    out_ref[320:384, :] = total.astype(bf16)


def fold(parts):
    rank = parts[0].shape[1]
    return pl.pallas_call(
        fold_kernel,
        in_specs=[VMEM] * len(parts),
        out_specs=VMEM,
        out_shape=jax.ShapeDtypeStruct((384, rank), bf16),
        compiler_params=params(),
        name="fold",
    )(*parts)


def group_kernel(order_ref, skel_ref, *refs):
    out_ref = refs[-1]
    parts = refs[:-1]
    rank = out_ref.shape[1]
    total = jnp.zeros((64, rank), f32)
    found = jnp.zeros((16, rank), f32)
    skeleton = skel_ref[0]
    for z, ref in enumerate(parts):
        total = total + ref[320:384, :].astype(f32)
        for x in range(4):
            hot = one_hot(skeleton, rank, order_ref[z * 4 + x] * rank)
            found = found + dot(ref[x * 80 + 64 : x * 80 + 80, :], hot)
    out_ref[0:64, :] = total.astype(bf16)
    out_ref[64:80, :] = found.astype(bf16)


def group_pass(order, group_skeleton, tx_index, parts):
    rank = parts[0].shape[1]
    own = lax.dynamic_slice_in_dim(group_skeleton, tx_index, 1, 0)[None]
    return pl.pallas_call(
        group_kernel,
        in_specs=[SMEM] + [VMEM] * 5,
        out_specs=VMEM,
        out_shape=jax.ShapeDtypeStruct((80, rank), bf16),
        compiler_params=params(),
        name="group_pass",
    )(order, own, *parts)


def far_kernel(slot_ref, own_ref, p0, p1, p2, p3, out_ref, pool):
    for z, ref in enumerate((p0, p1, p2, p3)):
        for x in range(4):
            pool[z * 4 + x] = ref[x * 80 : (x + 1) * 80, :]
    target = target_features(own_ref[64:80, :].astype(f32))
    total = jnp.zeros(out_ref.shape, f32)
    for k in range(slot_ref.shape[0]):
        slot = slot_ref[k]
        left = source_features(pool[slot, 64:80, :].astype(f32))
        total = total + dot(pool[slot, 0:64, :], entries(dot(left, target)))
    out_ref[...] = total * LN2


def far_pass(slots, own, parts):
    rank = own.shape[1]
    return pl.pallas_call(
        far_kernel,
        in_specs=[SMEM] + [VMEM] * 5,
        out_specs=VMEM,
        out_shape=jax.ShapeDtypeStruct((64, rank), f32),
        scratch_shapes=[pltpu.VMEM((16, 80, rank), bf16)],
        compiler_params=params(),
        name="far_pass",
    )(slots, own, *parts)


def down_kernel(far_ref, node_transfer_ref, transfer_ref, down_ref, near_ref, own_ref, *refs):
    out_ref, potential = refs[-2:]
    others = refs[:-2]

    @pl.when(pl.program_id(0) == 0)
    def _():
        target = target_features(own_ref[64:80, :].astype(f32))
        total = jnp.zeros(far_ref.shape, f32)
        for ref in others:
            left = source_features(ref[64:80, :].astype(f32))
            total = total + dot(ref[0:64, :], entries(dot(left, target)))
        group_potential = (total * LN2).astype(bf16)
        pushed = dot_nt(group_potential, node_transfer_ref[0])
        potential[...] = (far_ref[...] + pushed).astype(bf16)

    box_potential = dot_nt(potential[...], transfer_ref[0]).astype(bf16)
    out_ref[0] = (dot(box_potential, down_ref[0]) + near_ref[0] * LN2).astype(bf16)


def down_pass(far, node_transfer, box_transfer, down_basis, near, own, others):
    boxes, rank, leaf = down_basis.shape

    def whole(shape):
        return pl.BlockSpec(shape, lambda b: (0,) * len(shape))

    return pl.pallas_call(
        down_kernel,
        grid=(boxes,),
        in_specs=[
            whole((64, rank)),
            whole((1, rank, rank)),
            pl.BlockSpec((1, rank, rank), lambda b: (b, 0, 0)),
            pl.BlockSpec((1, rank, leaf), lambda b: (b, 0, 0)),
            pl.BlockSpec((1, 64, leaf), lambda b: (b, 0, 0)),
        ]
        + [whole((80, rank))] * (1 + len(others)),
        out_specs=pl.BlockSpec((1, 64, leaf), lambda b: (b, 0, 0)),
        out_shape=jax.ShapeDtypeStruct((boxes, 64, leaf), bf16),
        scratch_shapes=[pltpu.VMEM((64, rank), bf16)],
        compiler_params=params(),
        name="down_pass",
    )(far, node_transfer, box_transfer, down_basis, near, own, *others)


def shards(
    probes,
    points,
    up_basis,
    down_basis,
    box_skeleton,
    box_transfer,
    node_skeleton,
    node_transfer,
    group_skeleton,
    near_list,
    node_list,
):
    boxes = probes.shape[0]
    n_tx = lax.axis_size("tx")
    n_ty = lax.axis_size("ty")
    tx_index = lax.axis_index("tx")
    ty_index = lax.axis_index("ty")
    node = tx_index * n_ty + ty_index
    z_index, x_index = ty_index // 4, ty_index % 4
    base = ((node - 1) * boxes).astype(i32).reshape(1)

    packed, table = pack(near_list, base, probes, points)
    prev_box = lax.ppermute(packed, "ty", [(i, i + 1) for i in range(n_ty - 1)])
    next_box = lax.ppermute(packed, "ty", [(i + 1, i) for i in range(n_ty - 1)])
    count = table[5, 0]
    cut_one = jnp.minimum(table[5, 1], FIRST_UNITS)
    cut_two = jnp.minimum(count, SECOND_UNITS)

    own = up_pass(packed, up_basis, box_skeleton, box_transfer, node_skeleton, node_transfer)
    row = [own] + [
        lax.ppermute(own, "ty", [(i, (i // 4) * 4 + (i + s) % 4) for i in range(n_ty)]) for s in (1, 2, 3)
    ]
    near = near_part(FIRST_UNITS, jnp.stack([jnp.zeros_like(cut_one), cut_one]), table, packed)
    near, row = lax.optimization_barrier((near, row))

    folded = fold(row)
    parts = [folded] + [
        lax.ppermute(folded, "ty", [(i, (i + 4 * s) % n_ty) for i in range(n_ty)]) for s in (1, 2, 3)
    ]
    near = near_part(SECOND_UNITS, jnp.stack([cut_one, cut_two]), table, packed, (prev_box, next_box), near)
    near, parts = lax.optimization_barrier((near, parts))

    slots = jnp.arange(n_ty, dtype=i32)
    order = ((z_index - slots // 4) % 4) * 4 + (x_index - slots % 4) % 4
    group = group_pass(order.astype(i32), group_skeleton, tx_index, parts)
    others = [lax.ppermute(group, "tx", [(i, (i + s) % n_tx) for i in range(n_tx)]) for s in range(1, n_tx)]
    named = node_list[0] - tx_index * n_ty
    far_slots = ((z_index - named // 4) % 4) * 4 + (x_index - named % 4) % 4
    far = far_pass(far_slots.astype(i32), own, parts)
    near = near_part(SLOTS - SECOND_UNITS, jnp.stack([cut_two, count]), table, packed, (prev_box, next_box), near)
    near, others, far = lax.optimization_barrier((near, others, far))
    return down_pass(far, node_transfer, box_transfer, down_basis, near, group, others)


def solution(mesh):
    spec3 = P(("tx", "ty"), None, None)
    spec2 = P(("tx", "ty"), None)
    in_specs = (spec3, spec3, spec3, spec3, spec2, spec3, spec2, spec3, P(), spec2, spec2)
    return jax.shard_map(shards, mesh=mesh, in_specs=in_specs, out_specs=spec3, check_vma=False)
```

```python
import functools
import math

import jax
import jax.numpy as jnp
from jax import lax
from jax.experimental import pallas as pl
from jax.experimental.pallas import tpu as pltpu
from jax.sharding import PartitionSpec as P

bf16 = jnp.bfloat16
f32 = jnp.float32
i32 = jnp.int32

INV_LENGTH = 4.0
LN2 = math.log(2.0)
SCALE = INV_LENGTH / LN2
VMEM = pl.BlockSpec(memory_space=pltpu.VMEM)
SMEM = pl.BlockSpec(memory_space=pltpu.SMEM)
TILE_ROWS = 512
TILE_COLS = 1024
OWN_UNITS = 3
LATE_UNITS = 2
FIRST_UNITS = 1
LAST_AT = OWN_UNITS + LATE_UNITS
LAST_UNITS = 12
COLUMNS = LAST_AT + LAST_UNITS
SIDE, BOX, LIVE, OPENS, CLOSES, PREV, OWN, NEXT = range(8)


def params(mib=62):
    return pltpu.CompilerParams(vmem_limit_bytes=mib * 2**20)


SMALL = pl.CostEstimate(flops=1024, bytes_accessed=1024, transcendentals=0)


def split_points(points):
    scaled = (points - 0.5) * SCALE
    high = scaled.astype(bf16)
    low = (scaled - high.astype(f32)).astype(bf16)
    return high, low


def norm_rows(pair, one_first):
    high = pair[:8]
    low = pair[8:]
    full = high + low
    norm = jnp.sum(full * full, axis=0, keepdims=True)
    first = norm.astype(bf16).astype(f32)
    rest = norm - first
    second = rest.astype(bf16).astype(f32)
    third = rest - second
    row = lax.broadcasted_iota(i32, high.shape, 0)
    base = 3 if one_first else 0
    ones = 0 if one_first else 3
    out = jnp.where((row >= ones) & (row < ones + 3), 1.0, 0.0)
    out = jnp.where(row == base, first, out)
    out = jnp.where(row == base + 1, second, out)
    return jnp.where(row == base + 2, third, out)


def source_features(pair):
    high = pair[:8] * -2.0
    low = pair[8:] * -2.0
    return jnp.concatenate([high, low, high, norm_rows(pair, False)], axis=0).T.astype(bf16)


def target_features(pair):
    high = pair[:8]
    return jnp.concatenate([high, high, pair[8:], norm_rows(pair, True)], axis=0).astype(bf16)


def entries(squared):
    squared = jnp.maximum(squared, 1e-12)
    scaled = squared * lax.rsqrt(squared)
    return (scaled * jnp.exp2(-scaled)).astype(bf16)


def dot(a, b):
    return jnp.dot(a, b, preferred_element_type=f32)


def dot_nt(a, b):
    return lax.dot_general(a, b, (((1,), (1,)), ((), ())), preferred_element_type=f32)


def pack_kernel(near_ref, base_ref, probes_ref, points_ref, out_ref, table_ref):
    b = pl.program_id(0)
    out_ref[0, :64, :] = probes_ref[0]
    high, low = split_points(points_ref[0])
    out_ref[0, 64:80, :] = jnp.concatenate([high.astype(f32), low.astype(f32)], axis=0).astype(bf16)

    @pl.when(b == 0)
    def _():
        write_table(near_ref, base_ref, table_ref)


def write_table(near_ref, base_ref, table_ref):
    boxes, width = near_ref.shape
    for column in range(COLUMNS):
        table_ref[SIDE, column] = i32(1)
        table_ref[BOX, column] = i32(boxes - 1)
        for row in (LIVE, OPENS, CLOSES, PREV, OWN, NEXT):
            table_ref[row, column] = i32(0)

    units = []
    for box in range(boxes):
        for entry in range(width):
            named = near_ref[box, entry]
            slot = jnp.clip(named - base_ref[0], 0, 3 * boxes - 1)
            side = (slot >= boxes).astype(i32) + (slot >= 2 * boxes).astype(i32)
            units.append((box, named >= 0, side, slot - side * boxes))

    def put(column, when, box, side, index, hold):
        hold = [jnp.where(when & (side == k), index, hold[k]) for k in range(3)]

        @pl.when(when)
        def _():
            table_ref[SIDE, column] = side
            table_ref[BOX, column] = i32(box)
            table_ref[LIVE, column] = i32(1)
            for k, row in enumerate((PREV, OWN, NEXT)):
                table_ref[row, column] = hold[k]

        return hold

    zero = i32(0)
    own_rank = zero
    rest_rank = zero
    last_column = i32(LAST_AT)
    own_hold, late_hold, last_hold = [zero] * 3, [zero] * 3, [zero] * 3
    for box in range(boxes):
        opened = last_column
        for _, live, side, index in units[box * width : (box + 1) * width]:
            early = live & (side == 1) & (own_rank < OWN_UNITS)
            own_hold = put(own_rank, early, box, side, index, own_hold)
            own_rank = own_rank + early.astype(i32)
            rest = live & jnp.logical_not(early)
            late = rest & (rest_rank < LATE_UNITS)
            late_hold = put(OWN_UNITS + rest_rank, late, box, side, index, late_hold)
            rest_rank = rest_rank + rest.astype(i32)
            last = rest & jnp.logical_not(late)
            last_hold = put(last_column, last, box, side, index, last_hold)
            last_column = last_column + last.astype(i32)
        bare = last_column == opened

        @pl.when(bare)
        def _(column=last_column, box=box, hold=tuple(last_hold)):
            table_ref[BOX, column] = i32(box)
            for k, row in enumerate((PREV, OWN, NEXT)):
                table_ref[row, column] = hold[k]

        last_column = last_column + bare.astype(i32)
        table_ref[OPENS, opened] = i32(1)
        table_ref[CLOSES, last_column - 1] = i32(1)


def pack(near_list, base, probes, points):
    boxes, count, leaf = probes.shape
    return pl.pallas_call(
        pack_kernel,
        grid=(boxes,),
        in_specs=[
            SMEM,
            SMEM,
            pl.BlockSpec((1, count, leaf), lambda b: (b, 0, 0)),
            pl.BlockSpec((1, 8, leaf), lambda b: (b, 0, 0)),
        ],
        out_specs=[pl.BlockSpec((1, count + 16, leaf), lambda b: (b, 0, 0)), SMEM],
        out_shape=[
            jax.ShapeDtypeStruct((boxes, count + 16, leaf), bf16),
            jax.ShapeDtypeStruct((8, COLUMNS), i32),
        ],
        compiler_params=params(),
        name="pack",
    )(near_list, base, probes, points)


def one_hot(index_row, size, offset=0):
    rows = lax.broadcasted_iota(i32, (size, index_row.shape[1]), 0) + offset
    return jnp.where(rows == index_row, 1.0, 0.0).astype(bf16)


def up_kernel(packed_ref, up_ref, box_skel_ref, transfer_ref, node_skel_ref, node_transfer_ref, out_ref, acc, pool):
    b = pl.program_id(0)
    boxes = pl.num_programs(0)
    rank = up_ref.shape[1]
    leaf = up_ref.shape[2]

    @pl.when(b == 0)
    def _():
        acc[...] = jnp.zeros_like(acc)

    weights = dot_nt(packed_ref[0, :64, :], up_ref[0]).astype(bf16)
    acc[...] += dot(weights, transfer_ref[0])
    pool[b] = dot(packed_ref[0, 64:80, :], one_hot(box_skel_ref[pl.ds(b, 1), :], leaf)).astype(bf16)

    @pl.when(b == boxes - 1)
    def _():
        node_weight = acc[...].astype(bf16)
        out_ref[0:64, :] = node_weight
        found = jnp.zeros((16, rank), f32)
        for k in range(pool.shape[0]):
            found = found + dot(pool[k], one_hot(node_skel_ref[...], rank, k * rank))
        out_ref[64:80, :] = found.astype(bf16)
        out_ref[80:144, :] = dot(node_weight, node_transfer_ref[0]).astype(bf16)


def up_pass(packed, up_basis, box_skeleton, box_transfer, node_skeleton, node_transfer):
    boxes, rows, leaf = packed.shape
    rank = up_basis.shape[1]
    return pl.pallas_call(
        up_kernel,
        grid=(boxes,),
        in_specs=[
            pl.BlockSpec((1, rows, leaf), lambda b: (b, 0, 0)),
            pl.BlockSpec((1, rank, leaf), lambda b: (b, 0, 0)),
            pl.BlockSpec((boxes, rank), lambda b: (0, 0)),
            pl.BlockSpec((1, rank, rank), lambda b: (b, 0, 0)),
            pl.BlockSpec((1, rank), lambda b: (0, 0)),
            pl.BlockSpec((1, rank, rank), lambda b: (0, 0, 0)),
        ],
        out_specs=pl.BlockSpec((144, rank), lambda b: (0, 0)),
        out_shape=jax.ShapeDtypeStruct((144, rank), bf16),
        scratch_shapes=[pltpu.VMEM((64, rank), f32), pltpu.VMEM((boxes, 16, rank), bf16)],
        compiler_params=params(),
        name="up_pass",
    )(packed, up_basis, box_skeleton, box_transfer, node_skeleton, node_transfer)


def load_source(table, column, sources, held, left):
    side = table[SIDE, column]
    for k, ref in sources:

        @pl.when(side == k)
        def _(ref=ref):
            held[...] = ref[0, :64, :]
            left[...] = source_features(ref[0, 64:80, :].astype(f32))


def near_tile(held, left, right, write):
    leaf = left.shape[0]

    def columns(j, carry):
        cols = pl.ds(pl.multiple_of(j * TILE_COLS, TILE_COLS), TILE_COLS)
        total = jnp.zeros((held.shape[0], TILE_COLS), f32)
        for k in range(leaf // TILE_ROWS):
            rows = slice(k * TILE_ROWS, (k + 1) * TILE_ROWS)
            block = entries(dot(left[rows, :], right[:, cols]))
            total = total + dot(held[:, rows], block)
        write(cols, total)
        return carry

    lax.fori_loop(0, leaf // TILE_COLS, columns, 0)


def early_kernel(start, sides, table, *refs):
    sources = refs[: len(sides)]
    target_ref, out_ref, held, left, right = refs[len(sides) :]
    column = pl.program_id(0) + start

    @pl.when(table[LIVE, column] == 1)
    def _():
        load_source(table, column, list(zip(sides, sources)), held, left)
        right[...] = target_features(target_ref[0].astype(f32))

        def write(cols, total):
            out_ref[0, :, cols] = total

        near_tile(held, left, right, write)


def source_specs(start, sides, rows, leaf):
    def spec(row):
        return pl.BlockSpec((1, rows, leaf), lambda i, table: (table[row, i + start], 0, 0))

    target = pl.BlockSpec((1, 16, leaf), lambda i, table: (table[BOX, i + start], 4, 0))
    return [spec((PREV, OWN, NEXT)[k]) for k in sides] + [target]


def tile_scratch(leaf):
    return [pltpu.VMEM((64, leaf), bf16), pltpu.VMEM((leaf, 32), bf16), pltpu.VMEM((32, leaf), bf16)]


def near_early(start, units, table, packed, halo=None):
    _, rows, leaf = packed.shape
    sides = (1,) if halo is None else (0, 1, 2)
    arrays = (packed,) if halo is None else (halo[0], packed, halo[1])
    return pl.pallas_call(
        functools.partial(early_kernel, start, sides),
        grid_spec=pltpu.PrefetchScalarGridSpec(
            num_scalar_prefetch=1,
            grid=(units,),
            in_specs=source_specs(start, sides, rows, leaf),
            out_specs=pl.BlockSpec((1, 64, leaf), lambda i, table: (i, 0, 0)),
            scratch_shapes=tile_scratch(leaf),
        ),
        out_shape=jax.ShapeDtypeStruct((units, 64, leaf), f32),
        compiler_params=params(40),
        cost_estimate=SMALL,
        name="near_early",
    )(table, *arrays, packed)


def last_kernel(sides, table, *refs):
    sources = refs[: len(sides)]
    target_ref, potential_ref, transfer_ref, down_ref, *refs = refs[len(sides) :]
    *early, out_ref, held, left, right, total_ref = refs
    column = pl.program_id(0) + LAST_AT
    box = table[BOX, column]

    @pl.when(table[OPENS, column] == 1)
    def _():
        total_ref[...] = jnp.zeros_like(total_ref)
        at = 0
        for ref in early:
            for k in range(ref.shape[0]):

                @pl.when((table[LIVE, at] == 1) & (table[BOX, at] == box))
                def _(ref=ref, k=k):
                    total_ref[...] += ref[k]

                at += 1

    @pl.when(table[LIVE, column] == 1)
    def _():
        load_source(table, column, list(zip(sides, sources)), held, left)
        right[...] = target_features(target_ref[0].astype(f32))

        def write(cols, total):
            total_ref[:, cols] += total

        near_tile(held, left, right, write)

    @pl.when(table[CLOSES, column] == 1)
    def _():
        box_potential = dot_nt(potential_ref[...], transfer_ref[0]).astype(bf16)
        out_ref[0] = (dot(box_potential, down_ref[0]) + total_ref[...] * LN2).astype(bf16)


def near_last(table, packed, halo, potential, box_transfer, down_basis, early):
    boxes, rows, leaf = packed.shape
    rank = down_basis.shape[1]
    sides = (0, 1, 2)

    def whole(shape):
        return pl.BlockSpec(shape, lambda i, table: (0,) * len(shape))

    def by_box(shape):
        return pl.BlockSpec(shape, lambda i, table: (table[BOX, i + LAST_AT], 0, 0))

    return pl.pallas_call(
        functools.partial(last_kernel, sides),
        grid_spec=pltpu.PrefetchScalarGridSpec(
            num_scalar_prefetch=1,
            grid=(LAST_UNITS,),
            in_specs=source_specs(LAST_AT, sides, rows, leaf)
            + [whole((64, rank)), by_box((1, rank, rank)), by_box((1, rank, leaf))]
            + [whole(part.shape) for part in early],
            out_specs=by_box((1, 64, leaf)),
            scratch_shapes=tile_scratch(leaf) + [pltpu.VMEM((64, leaf), f32)],
        ),
        out_shape=jax.ShapeDtypeStruct((boxes, 64, leaf), bf16),
        compiler_params=params(40),
        cost_estimate=SMALL,
        name="near_last",
    )(table, halo[0], packed, halo[1], packed, potential, box_transfer, down_basis, *early)


def fold_kernel(*refs):
    out_ref = refs[-1]
    total = jnp.zeros((64, out_ref.shape[1]), f32)
    for k, ref in enumerate(refs[:-1]):
        out_ref[k * 80 : (k + 1) * 80, :] = ref[0:80, :]
        total = total + ref[80:144, :].astype(f32)
    out_ref[320:384, :] = total.astype(bf16)


def fold(parts):
    rank = parts[0].shape[1]
    return pl.pallas_call(
        fold_kernel,
        in_specs=[VMEM] * len(parts),
        out_specs=VMEM,
        out_shape=jax.ShapeDtypeStruct((384, rank), bf16),
        compiler_params=params(16),
        name="fold",
    )(*parts)


def group_kernel(order_ref, skel_ref, *refs):
    out_ref = refs[-1]
    parts = refs[:-1]
    rank = out_ref.shape[1]
    total = jnp.zeros((64, rank), f32)
    found = jnp.zeros((16, rank), f32)
    skeleton = skel_ref[0]
    for z, ref in enumerate(parts):
        total = total + ref[320:384, :].astype(f32)
        for x in range(4):
            hot = one_hot(skeleton, rank, order_ref[z * 4 + x] * rank)
            found = found + dot(ref[x * 80 + 64 : x * 80 + 80, :], hot)
    out_ref[0:64, :] = total.astype(bf16)
    out_ref[64:80, :] = found.astype(bf16)


def group_pass(order, group_skeleton, tx_index, parts):
    rank = parts[0].shape[1]
    own = lax.dynamic_slice_in_dim(group_skeleton, tx_index, 1, 0)[None]
    return pl.pallas_call(
        group_kernel,
        in_specs=[SMEM] + [VMEM] * 5,
        out_specs=VMEM,
        out_shape=jax.ShapeDtypeStruct((80, rank), bf16),
        compiler_params=params(16),
        name="group_pass",
    )(order, own, *parts)


def far_kernel(slot_ref, own_ref, node_transfer_ref, group_ref, *refs):
    parts, others = refs[:4], refs[4:-2]
    out_ref, pool = refs[-2:]
    for z, ref in enumerate(parts):
        for x in range(4):
            pool[z * 4 + x] = ref[x * 80 : (x + 1) * 80, :]
    target = target_features(group_ref[64:80, :].astype(f32))
    total = jnp.zeros(out_ref.shape, f32)
    for ref in others:
        left = source_features(ref[64:80, :].astype(f32))
        total = total + dot(ref[0:64, :], entries(dot(left, target)))
    group_potential = (total * LN2).astype(bf16)
    target = target_features(own_ref[64:80, :].astype(f32))
    total = jnp.zeros(out_ref.shape, f32)
    for k in range(slot_ref.shape[0]):
        slot = slot_ref[k]
        left = source_features(pool[slot, 64:80, :].astype(f32))
        total = total + dot(pool[slot, 0:64, :], entries(dot(left, target)))
    out_ref[...] = (total * LN2 + dot_nt(group_potential, node_transfer_ref[0])).astype(bf16)


def far_pass(slots, own, node_transfer, group, parts, others):
    rank = own.shape[1]
    return pl.pallas_call(
        far_kernel,
        in_specs=[SMEM] + [VMEM] * (3 + len(parts) + len(others)),
        out_specs=VMEM,
        out_shape=jax.ShapeDtypeStruct((64, rank), bf16),
        scratch_shapes=[pltpu.VMEM((16, 80, rank), bf16)],
        compiler_params=params(16),
        cost_estimate=SMALL,
        name="far_pass",
    )(slots, own, node_transfer, group, *parts, *others)


def shards(
    probes,
    points,
    up_basis,
    down_basis,
    box_skeleton,
    box_transfer,
    node_skeleton,
    node_transfer,
    group_skeleton,
    near_list,
    node_list,
):
    boxes = probes.shape[0]
    n_tx = lax.axis_size("tx")
    n_ty = lax.axis_size("ty")
    tx_index = lax.axis_index("tx")
    ty_index = lax.axis_index("ty")
    node = tx_index * n_ty + ty_index
    z_index, x_index = ty_index // 4, ty_index % 4
    base = ((node - 1) * boxes).astype(i32).reshape(1)

    packed, table = pack(near_list, base, probes, points)
    prev_box = lax.ppermute(packed, "ty", [(i, i + 1) for i in range(n_ty - 1)])
    next_box = lax.ppermute(packed, "ty", [(i + 1, i) for i in range(n_ty - 1)])

    own = up_pass(packed, up_basis, box_skeleton, box_transfer, node_skeleton, node_transfer)
    row = [own] + [
        lax.ppermute(own, "ty", [(i, (i // 4) * 4 + (i + s) % 4) for i in range(n_ty)]) for s in (1, 2, 3)
    ]
    first = near_early(0, FIRST_UNITS, table, packed)
    first, row = lax.optimization_barrier((first, row))

    folded = fold(row)
    parts = [folded] + [
        lax.ppermute(folded, "ty", [(i, (i + 4 * s) % n_ty) for i in range(n_ty)]) for s in (1, 2, 3)
    ]
    second_table, parts[0] = lax.optimization_barrier((table, folded))
    second = near_early(FIRST_UNITS, OWN_UNITS - FIRST_UNITS, second_table, packed)
    second, parts = lax.optimization_barrier((second, parts))

    slots = jnp.arange(n_ty, dtype=i32)
    order = ((z_index - slots // 4) % 4) * 4 + (x_index - slots % 4) % 4
    group = group_pass(order.astype(i32), group_skeleton, tx_index, parts)
    others = [lax.ppermute(group, "tx", [(i, (i + s) % n_tx) for i in range(n_tx)]) for s in range(1, n_tx)]
    named = node_list[0] - tx_index * n_ty
    far_slots = ((z_index - named // 4) % 4) * 4 + (x_index - named % 4) % 4
    halo = (prev_box, next_box)
    third_table, group = lax.optimization_barrier((table, group))
    third = near_early(OWN_UNITS, LATE_UNITS, third_table, packed, halo)
    third, others = lax.optimization_barrier((third, others))
    potential = far_pass(far_slots.astype(i32), own, node_transfer, group, parts, others)
    return near_last(table, packed, halo, potential, box_transfer, down_basis, (first, second, third))


def solution(mesh):
    spec3 = P(("tx", "ty"), None, None)
    spec2 = P(("tx", "ty"), None)
    in_specs = (spec3, spec3, spec3, spec3, spec2, spec3, spec2, spec3, P(), spec2, spec2)
    return jax.shard_map(shards, mesh=mesh, in_specs=in_specs, out_specs=spec3, check_vma=False)
```

```python
import functools
import math

import jax
import jax.numpy as jnp
from jax import lax
from jax.experimental import pallas as pl
from jax.experimental.pallas import tpu as pltpu
from jax.sharding import PartitionSpec as P

bf16 = jnp.bfloat16
f32 = jnp.float32
i32 = jnp.int32

INV_LENGTH = 4.0
LN2 = math.log(2.0)
SCALE = INV_LENGTH / LN2
VMEM = pl.BlockSpec(memory_space=pltpu.VMEM)
SMEM = pl.BlockSpec(memory_space=pltpu.SMEM)
TILE_ROWS = 512
TILE_COLS = 1024
OWN_UNITS = 3
LATE_UNITS = 7
FIRST_LATE = 3
GROUP_ROWS = 256
LAST_AT = OWN_UNITS + LATE_UNITS
LAST_UNITS = 12
COLUMNS = LAST_AT + LAST_UNITS
SIDE, BOX, LIVE, OPENS, CLOSES, PREV, OWN, NEXT = range(8)


def params(mib=62):
    return pltpu.CompilerParams(vmem_limit_bytes=mib * 2**20)


SMALL = pl.CostEstimate(flops=1024, bytes_accessed=1024, transcendentals=0)


def split_points(points):
    scaled = (points - 0.5) * SCALE
    high = scaled.astype(bf16)
    low = (scaled - high.astype(f32)).astype(bf16)
    return high, low


def norm_rows(pair, one_first):
    high = pair[:8]
    low = pair[8:]
    full = high + low
    norm = jnp.sum(full * full, axis=0, keepdims=True)
    first = norm.astype(bf16).astype(f32)
    rest = norm - first
    second = rest.astype(bf16).astype(f32)
    third = rest - second
    row = lax.broadcasted_iota(i32, high.shape, 0)
    base = 3 if one_first else 0
    ones = 0 if one_first else 3
    out = jnp.where((row >= ones) & (row < ones + 3), 1.0, 0.0)
    out = jnp.where(row == base, first, out)
    out = jnp.where(row == base + 1, second, out)
    return jnp.where(row == base + 2, third, out)


def source_features(pair):
    high = pair[:8] * -2.0
    low = pair[8:] * -2.0
    return jnp.concatenate([high, low, high, norm_rows(pair, False)], axis=0).T.astype(bf16)


def target_features(pair):
    high = pair[:8]
    return jnp.concatenate([high, high, pair[8:], norm_rows(pair, True)], axis=0).astype(bf16)


def entries(squared):
    squared = jnp.maximum(squared, 1e-12)
    scaled = squared * lax.rsqrt(squared)
    return (scaled * jnp.exp2(-scaled)).astype(bf16)


def dot(a, b):
    return jnp.dot(a, b, preferred_element_type=f32)


def dot_nt(a, b):
    return lax.dot_general(a, b, (((1,), (1,)), ((), ())), preferred_element_type=f32)


def pack_kernel(near_ref, base_ref, probes_ref, points_ref, out_ref, table_ref):
    b = pl.program_id(0)
    out_ref[0, :64, :] = probes_ref[0]
    high, low = split_points(points_ref[0])
    out_ref[0, 64:80, :] = jnp.concatenate([high.astype(f32), low.astype(f32)], axis=0).astype(bf16)

    @pl.when(b == 0)
    def _():
        write_table(near_ref, base_ref, table_ref)


def write_table(near_ref, base_ref, table_ref):
    boxes, width = near_ref.shape
    for column in range(COLUMNS):
        table_ref[SIDE, column] = i32(1)
        table_ref[BOX, column] = i32(boxes - 1)
        for row in (LIVE, OPENS, CLOSES, PREV, OWN, NEXT):
            table_ref[row, column] = i32(0)

    units = []
    for box in range(boxes):
        for entry in range(width):
            named = near_ref[box, entry]
            slot = jnp.clip(named - base_ref[0], 0, 3 * boxes - 1)
            side = (slot >= boxes).astype(i32) + (slot >= 2 * boxes).astype(i32)
            units.append((box, named >= 0, side, slot - side * boxes))

    def put(column, when, box, side, index, hold):
        hold = [jnp.where(when & (side == k), index, hold[k]) for k in range(3)]

        @pl.when(when)
        def _():
            table_ref[SIDE, column] = side
            table_ref[BOX, column] = i32(box)
            table_ref[LIVE, column] = i32(1)
            for k, row in enumerate((PREV, OWN, NEXT)):
                table_ref[row, column] = hold[k]

        return hold

    zero = i32(0)
    own_rank = zero
    rest_rank = zero
    last_column = i32(LAST_AT)
    own_hold, late_hold, last_hold = [zero] * 3, [zero] * 3, [zero] * 3
    for box in range(boxes):
        opened = last_column
        for _, live, side, index in units[box * width : (box + 1) * width]:
            early = live & (side == 1) & (own_rank < OWN_UNITS)
            own_hold = put(own_rank, early, box, side, index, own_hold)
            own_rank = own_rank + early.astype(i32)
            rest = live & jnp.logical_not(early)
            late = rest & (rest_rank < LATE_UNITS)
            late_hold = put(OWN_UNITS + rest_rank, late, box, side, index, late_hold)
            rest_rank = rest_rank + rest.astype(i32)
            last = rest & jnp.logical_not(late)
            last_hold = put(last_column, last, box, side, index, last_hold)
            last_column = last_column + last.astype(i32)
        bare = last_column == opened

        @pl.when(bare)
        def _(column=last_column, box=box, hold=tuple(last_hold)):
            table_ref[BOX, column] = i32(box)
            for k, row in enumerate((PREV, OWN, NEXT)):
                table_ref[row, column] = hold[k]

        last_column = last_column + bare.astype(i32)
        table_ref[OPENS, opened] = i32(1)
        table_ref[CLOSES, last_column - 1] = i32(1)


def pack(near_list, base, probes, points):
    boxes, count, leaf = probes.shape
    return pl.pallas_call(
        pack_kernel,
        grid=(boxes,),
        in_specs=[
            SMEM,
            SMEM,
            pl.BlockSpec((1, count, leaf), lambda b: (b, 0, 0)),
            pl.BlockSpec((1, 8, leaf), lambda b: (b, 0, 0)),
        ],
        out_specs=[pl.BlockSpec((1, count + 16, leaf), lambda b: (b, 0, 0)), SMEM],
        out_shape=[
            jax.ShapeDtypeStruct((boxes, count + 16, leaf), bf16),
            jax.ShapeDtypeStruct((8, COLUMNS), i32),
        ],
        compiler_params=params(),
        name="pack",
    )(near_list, base, probes, points)


def one_hot(index_row, size, offset=0):
    rows = lax.broadcasted_iota(i32, (size, index_row.shape[1]), 0) + offset
    return jnp.where(rows == index_row, 1.0, 0.0).astype(bf16)


def up_kernel(packed_ref, up_ref, box_skel_ref, transfer_ref, node_skel_ref, node_transfer_ref, out_ref, acc, pool):
    b = pl.program_id(0)
    boxes = pl.num_programs(0)
    rank = up_ref.shape[1]
    leaf = up_ref.shape[2]

    @pl.when(b == 0)
    def _():
        acc[...] = jnp.zeros_like(acc)

    weights = dot_nt(packed_ref[0, :64, :], up_ref[0]).astype(bf16)
    acc[...] += dot(weights, transfer_ref[0])
    pool[b] = dot(packed_ref[0, 64:80, :], one_hot(box_skel_ref[pl.ds(b, 1), :], leaf)).astype(bf16)

    @pl.when(b == boxes - 1)
    def _():
        node_weight = acc[...].astype(bf16)
        out_ref[0:64, :] = node_weight
        found = jnp.zeros((16, rank), f32)
        for k in range(pool.shape[0]):
            found = found + dot(pool[k], one_hot(node_skel_ref[...], rank, k * rank))
        out_ref[64:80, :] = found.astype(bf16)
        out_ref[80:144, :] = dot(node_weight, node_transfer_ref[0]).astype(bf16)


def up_pass(packed, up_basis, box_skeleton, box_transfer, node_skeleton, node_transfer):
    boxes, rows, leaf = packed.shape
    rank = up_basis.shape[1]
    return pl.pallas_call(
        up_kernel,
        grid=(boxes,),
        in_specs=[
            pl.BlockSpec((1, rows, leaf), lambda b: (b, 0, 0)),
            pl.BlockSpec((1, rank, leaf), lambda b: (b, 0, 0)),
            pl.BlockSpec((boxes, rank), lambda b: (0, 0)),
            pl.BlockSpec((1, rank, rank), lambda b: (b, 0, 0)),
            pl.BlockSpec((1, rank), lambda b: (0, 0)),
            pl.BlockSpec((1, rank, rank), lambda b: (0, 0, 0)),
        ],
        out_specs=pl.BlockSpec((144, rank), lambda b: (0, 0)),
        out_shape=jax.ShapeDtypeStruct((144, rank), bf16),
        scratch_shapes=[pltpu.VMEM((64, rank), f32), pltpu.VMEM((boxes, 16, rank), bf16)],
        compiler_params=params(),
        name="up_pass",
    )(packed, up_basis, box_skeleton, box_transfer, node_skeleton, node_transfer)


def load_source(table, column, sources, held, left):
    side = table[SIDE, column]
    for k, ref in sources:

        @pl.when(side == k)
        def _(ref=ref):
            held[...] = ref[0, :64, :]
            left[...] = source_features(ref[0, 64:80, :].astype(f32))


def near_tile(held, left, right, write):
    leaf = left.shape[0]

    def columns(j, carry):
        cols = pl.ds(pl.multiple_of(j * TILE_COLS, TILE_COLS), TILE_COLS)
        total = jnp.zeros((held.shape[0], TILE_COLS), f32)
        for k in range(leaf // TILE_ROWS):
            rows = slice(k * TILE_ROWS, (k + 1) * TILE_ROWS)
            block = entries(dot(left[rows, :], right[:, cols]))
            total = total + dot(held[:, rows], block)
        write(cols, total)
        return carry

    lax.fori_loop(0, leaf // TILE_COLS, columns, 0)


def early_kernel(start, sides, table, *refs):
    sources = refs[: len(sides)]
    target_ref, out_ref, held, left, right = refs[len(sides) :]
    column = pl.program_id(0) + start

    @pl.when(table[LIVE, column] == 1)
    def _():
        load_source(table, column, list(zip(sides, sources)), held, left)
        right[...] = target_features(target_ref[0].astype(f32))

        def write(cols, total):
            out_ref[0, :, cols] = total

        near_tile(held, left, right, write)


def source_specs(start, sides, rows, leaf):
    def spec(row):
        return pl.BlockSpec((1, rows, leaf), lambda i, table: (table[row, i + start], 0, 0))

    target = pl.BlockSpec((1, 16, leaf), lambda i, table: (table[BOX, i + start], 4, 0))
    return [spec((PREV, OWN, NEXT)[k]) for k in sides] + [target]


def tile_scratch(leaf):
    return [pltpu.VMEM((64, leaf), bf16), pltpu.VMEM((leaf, 32), bf16), pltpu.VMEM((32, leaf), bf16)]


def near_early(start, units, table, packed, halo=None):
    _, rows, leaf = packed.shape
    sides = (1,) if halo is None else (0, 1, 2)
    arrays = (packed,) if halo is None else (halo[0], packed, halo[1])
    return pl.pallas_call(
        functools.partial(early_kernel, start, sides),
        grid_spec=pltpu.PrefetchScalarGridSpec(
            num_scalar_prefetch=1,
            grid=(units,),
            in_specs=source_specs(start, sides, rows, leaf),
            out_specs=pl.BlockSpec((1, 64, leaf), lambda i, table: (i, 0, 0)),
            scratch_shapes=tile_scratch(leaf),
        ),
        out_shape=jax.ShapeDtypeStruct((units, 64, leaf), f32),
        compiler_params=params(40),
        cost_estimate=SMALL,
        name="near_early",
    )(table, *arrays, packed)


def last_kernel(sides, table, *refs):
    sources = refs[: len(sides)]
    target_ref, potential_ref, transfer_ref, down_ref, *refs = refs[len(sides) :]
    *early, out_ref, held, left, right, total_ref = refs
    column = pl.program_id(0) + LAST_AT
    box = table[BOX, column]

    @pl.when(table[OPENS, column] == 1)
    def _():
        total_ref[...] = jnp.zeros_like(total_ref)
        at = 0
        for ref in early:
            for k in range(ref.shape[0]):

                @pl.when((table[LIVE, at] == 1) & (table[BOX, at] == box))
                def _(ref=ref, k=k):
                    total_ref[...] += ref[k]

                at += 1

    @pl.when(table[LIVE, column] == 1)
    def _():
        load_source(table, column, list(zip(sides, sources)), held, left)
        right[...] = target_features(target_ref[0].astype(f32))

        def write(cols, total):
            total_ref[:, cols] += total

        near_tile(held, left, right, write)

    @pl.when(table[CLOSES, column] == 1)
    def _():
        box_potential = dot_nt(potential_ref[...], transfer_ref[0]).astype(bf16)
        out_ref[0] = (dot(box_potential, down_ref[0]) + total_ref[...] * LN2).astype(bf16)


def near_last(table, packed, halo, potential, box_transfer, down_basis, early):
    boxes, rows, leaf = packed.shape
    rank = down_basis.shape[1]
    sides = (0, 1, 2)

    def whole(shape):
        return pl.BlockSpec(shape, lambda i, table: (0,) * len(shape))

    def by_box(shape):
        return pl.BlockSpec(shape, lambda i, table: (table[BOX, i + LAST_AT], 0, 0))

    return pl.pallas_call(
        functools.partial(last_kernel, sides),
        grid_spec=pltpu.PrefetchScalarGridSpec(
            num_scalar_prefetch=1,
            grid=(LAST_UNITS,),
            in_specs=source_specs(LAST_AT, sides, rows, leaf)
            + [whole((64, rank)), by_box((1, rank, rank)), by_box((1, rank, leaf))]
            + [whole(part.shape) for part in early],
            out_specs=by_box((1, 64, leaf)),
            scratch_shapes=tile_scratch(leaf) + [pltpu.VMEM((64, leaf), f32)],
        ),
        out_shape=jax.ShapeDtypeStruct((boxes, 64, leaf), bf16),
        compiler_params=params(40),
        cost_estimate=SMALL,
        name="near_last",
    )(table, halo[0], packed, halo[1], packed, potential, box_transfer, down_basis, *early)


def group_kernel(skel_ref, nodes_ref, out_ref):
    nodes, _, rank = nodes_ref.shape
    total = jnp.zeros((64, rank), f32)
    found = jnp.zeros((16, rank), f32)
    skeleton = skel_ref[0]
    for k in range(nodes):
        total = total + nodes_ref[k, 80:144, :].astype(f32)
        found = found + dot(nodes_ref[k, 64:80, :], one_hot(skeleton, rank, k * rank))
    out_ref[...] = jnp.zeros_like(out_ref)
    out_ref[0:64, :] = total.astype(bf16)
    out_ref[64:80, :] = found.astype(bf16)


def group_pass(group_skeleton, tx_index, nodes):
    rank = nodes.shape[2]
    own = lax.dynamic_slice_in_dim(group_skeleton, tx_index, 1, 0)[None]
    return pl.pallas_call(
        group_kernel,
        in_specs=[VMEM] * 2,
        out_specs=VMEM,
        out_shape=jax.ShapeDtypeStruct((GROUP_ROWS, rank), bf16),
        compiler_params=params(),
        name="group_pass",
    )(own, nodes)


def far_kernel(place_ref, list_ref, nodes_ref, groups_ref, node_transfer_ref, out_ref):
    tx_index, ty_index = place_ref[0], place_ref[1]
    target = target_features(groups_ref[tx_index, 64:80, :].astype(f32))
    total = jnp.zeros(out_ref.shape, f32)
    for k in range(groups_ref.shape[0]):
        left = source_features(groups_ref[k, 64:80, :].astype(f32))
        term = dot(groups_ref[k, 0:64, :], entries(dot(left, target)))
        total = total + jnp.where(k != tx_index, term, 0.0)
    group_potential = (total * LN2).astype(bf16)
    target = target_features(nodes_ref[ty_index, 64:80, :].astype(f32))
    total = jnp.zeros(out_ref.shape, f32)
    for k in range(list_ref.shape[1]):
        slot = jnp.clip(list_ref[0, k] - tx_index * nodes_ref.shape[0], 0, nodes_ref.shape[0] - 1)
        left = source_features(nodes_ref[slot, 64:80, :].astype(f32))
        total = total + dot(nodes_ref[slot, 0:64, :], entries(dot(left, target)))
    out_ref[...] = (total * LN2 + dot_nt(group_potential, node_transfer_ref[0])).astype(bf16)


def far_pass(place, node_list, nodes, groups, node_transfer):
    rank = nodes.shape[2]
    return pl.pallas_call(
        far_kernel,
        in_specs=[SMEM] * 2 + [VMEM] * 3,
        out_specs=VMEM,
        out_shape=jax.ShapeDtypeStruct((64, rank), bf16),
        compiler_params=params(),
        cost_estimate=SMALL,
        name="far_pass",
    )(place, node_list, nodes, groups, node_transfer)


def shards(
    probes,
    points,
    up_basis,
    down_basis,
    box_skeleton,
    box_transfer,
    node_skeleton,
    node_transfer,
    group_skeleton,
    near_list,
    node_list,
):
    boxes = probes.shape[0]
    n_tx = lax.axis_size("tx")
    n_ty = lax.axis_size("ty")
    tx_index = lax.axis_index("tx")
    ty_index = lax.axis_index("ty")
    node = tx_index * n_ty + ty_index
    base = 3 if one_first else 0
    ones = 0 if one_first else 3
    out = jnp.where((row >= ones) & (row < ones + 3), 1.0, 0.0)
    out = jnp.where(row == base, first, out)
    out = jnp.where(row == base + 1, second, out)
    return jnp.where(row == base + 2, third, out)


def source_features(pair):
    high = pair[:8] * -2.0
    low = pair[8:] * -2.0
    return jnp.concatenate([high, low, high, norm_rows(pair, False)], axis=0).T.astype(bf16)


def target_features(pair):
    high = pair[:8]
    return jnp.concatenate([high, high, pair[8:], norm_rows(pair, True)], axis=0).astype(bf16)


def entries(squared):
    squared = jnp.maximum(squared, 1e-12)
    scaled = squared * lax.rsqrt(squared)
    return (scaled * jnp.exp2(-scaled)).astype(bf16)


def dot(a, b):
    return jnp.dot(a, b, preferred_element_type=f32)


def dot_nt(a, b):
    return lax.dot_general(a, b, (((1,), (1,)), ((), ())), preferred_element_type=f32)


def pack_kernel(near_ref, base_ref, probes_ref, points_ref, out_ref, table_ref):
    b = pl.program_id(0)
    out_ref[0, :64, :] = probes_ref[0]
    high, low = split_points(points_ref[0])
    out_ref[0, 64:80, :] = jnp.concatenate([high.astype(f32), low.astype(f32)], axis=0).astype(bf16)

    @pl.when(b == 0)
    def _():
        write_table(near_ref, base_ref, table_ref)


def write_table(near_ref, base_ref, table_ref):
    boxes, width = near_ref.shape
    for column in range(COLUMNS):
        table_ref[SIDE, column] = i32(1)
        table_ref[BOX, column] = i32(boxes - 1)
        for row in (LIVE, OPENS, CLOSES, PREV, OWN, NEXT):
            table_ref[row, column] = i32(0)

    units = []
    for box in range(boxes):
        for entry in range(width):
            named = near_ref[box, entry]
            slot = jnp.clip(named - base_ref[0], 0, 3 * boxes - 1)
            side = (slot >= boxes).astype(i32) + (slot >= 2 * boxes).astype(i32)
            units.append((box, named >= 0, side, slot - side * boxes))

    def put(column, when, box, side, index, hold):
        hold = [jnp.where(when & (side == k), index, hold[k]) for k in range(3)]

        @pl.when(when)
        def _():
            table_ref[SIDE, column] = side
            table_ref[BOX, column] = i32(box)
            table_ref[LIVE, column] = i32(1)
            for k, row in enumerate((PREV, OWN, NEXT)):
                table_ref[row, column] = hold[k]

        return hold

    zero = i32(0)
    own_rank = zero
    rest_rank = zero
    last_column = i32(LAST_AT)
    own_hold, late_hold, last_hold = [zero] * 3, [zero] * 3, [zero] * 3
    for box in range(boxes):
        opened = last_column
        for _, live, side, index in units[box * width : (box + 1) * width]:
            early = live & (side == 1) & (own_rank < OWN_UNITS)
            own_hold = put(own_rank, early, box, side, index, own_hold)
            own_rank = own_rank + early.astype(i32)
            rest = live & jnp.logical_not(early)
            late = rest & (rest_rank < LATE_UNITS)
            late_hold = put(OWN_UNITS + rest_rank, late, box, side, index, late_hold)
            rest_rank = rest_rank + rest.astype(i32)
            last = rest & jnp.logical_not(late)
            last_hold = put(last_column, last, box, side, index, last_hold)
            last_column = last_column + last.astype(i32)
        bare = last_column == opened

        @pl.when(bare)
        def _(column=last_column, box=box, hold=tuple(last_hold)):
            table_ref[BOX, column] = i32(box)
            for k, row in enumerate((PREV, OWN, NEXT)):
                table_ref[row, column] = hold[k]

        last_column = last_column + bare.astype(i32)
        table_ref[OPENS, opened] = i32(1)
        table_ref[CLOSES, last_column - 1] = i32(1)


def pack(near_list, base, probes, points):
    boxes, count, leaf = probes.shape
    return pl.pallas_call(
        pack_kernel,
        grid=(boxes,),
        in_specs=[
            SMEM,
            SMEM,
            pl.BlockSpec((1, count, leaf), lambda b: (b, 0, 0)),
            pl.BlockSpec((1, 8, leaf), lambda b: (b, 0, 0)),
        ],
        out_specs=[pl.BlockSpec((1, count + 16, leaf), lambda b: (b, 0, 0)), SMEM],
        out_shape=[
            jax.ShapeDtypeStruct((boxes, count + 16, leaf), bf16),
            jax.ShapeDtypeStruct((8, COLUMNS), i32),
        ],
        compiler_params=params(),
        name="pack",
    )(near_list, base, probes, points)


def one_hot(index_row, size, offset=0):
    rows = lax.broadcasted_iota(i32, (size, index_row.shape[1]), 0) + offset
    return jnp.where(rows == index_row, 1.0, 0.0).astype(bf16)


def up_kernel(packed_ref, up_ref, box_skel_ref, transfer_ref, node_skel_ref, node_transfer_ref, out_ref, acc, pool):
    b = pl.program_id(0)
    boxes = pl.num_programs(0)
    rank = up_ref.shape[1]
    leaf = up_ref.shape[2]

    @pl.when(b == 0)
    def _():
        acc[...] = jnp.zeros_like(acc)

    weights = dot_nt(packed_ref[0, :64, :], up_ref[0]).astype(bf16)
    acc[...] += dot(weights, transfer_ref[0])
    pool[b] = dot(packed_ref[0, 64:80, :], one_hot(box_skel_ref[pl.ds(b, 1), :], leaf)).astype(bf16)

    @pl.when(b == boxes - 1)
    def _():
        node_weight = acc[...].astype(bf16)
        out_ref[0:64, :] = node_weight
        found = jnp.zeros((16, rank), f32)
        for k in range(pool.shape[0]):
            found = found + dot(pool[k], one_hot(node_skel_ref[...], rank, k * rank))
        out_ref[64:80, :] = found.astype(bf16)
        out_ref[80:144, :] = dot(node_weight, node_transfer_ref[0]).astype(bf16)


def up_pass(packed, up_basis, box_skeleton, box_transfer, node_skeleton, node_transfer):
    boxes, rows, leaf = packed.shape
    rank = up_basis.shape[1]
    return pl.pallas_call(
        up_kernel,
        grid=(boxes,),
        in_specs=[
            pl.BlockSpec((1, rows, leaf), lambda b: (b, 0, 0)),
            pl.BlockSpec((1, rank, leaf), lambda b: (b, 0, 0)),
            pl.BlockSpec((boxes, rank), lambda b: (0, 0)),
            pl.BlockSpec((1, rank, rank), lambda b: (b, 0, 0)),
            pl.BlockSpec((1, rank), lambda b: (0, 0)),
            pl.BlockSpec((1, rank, rank), lambda b: (0, 0, 0)),
        ],
        out_specs=pl.BlockSpec((144, rank), lambda b: (0, 0)),
        out_shape=jax.ShapeDtypeStruct((144, rank), bf16),
        scratch_shapes=[pltpu.VMEM((64, rank), f32), pltpu.VMEM((boxes, 16, rank), bf16)],
        compiler_params=params(),
        name="up_pass",
    )(packed, up_basis, box_skeleton, box_transfer, node_skeleton, node_transfer)


def load_source(table, column, sources, held, left):
    side = table[SIDE, column]
    for k, ref in sources:

        @pl.when(side == k)
        def _(ref=ref):
            held[...] = ref[0, :64, :]
            left[...] = source_features(ref[0, 64:80, :].astype(f32))


def near_tile(held, left, right, write):
    leaf = left.shape[0]

    def columns(j, carry):
        cols = pl.ds(pl.multiple_of(j * TILE_COLS, TILE_COLS), TILE_COLS)
        total = jnp.zeros((held.shape[0], TILE_COLS), f32)
        for k in range(leaf // TILE_ROWS):
            rows = slice(k * TILE_ROWS, (k + 1) * TILE_ROWS)
            block = entries(dot(left[rows, :], right[:, cols]))
            total = total + dot(held[:, rows], block)
        write(cols, total)
        return carry

    lax.fori_loop(0, leaf // TILE_COLS, columns, 0)


def early_kernel(start, sides, table, *refs):
    sources = refs[: len(sides)]
    target_ref, out_ref, held, left, right = refs[len(sides) :]
    column = pl.program_id(0) + start

    @pl.when(table[LIVE, column] == 1)
    def _():
        load_source(table, column, list(zip(sides, sources)), held, left)
        right[...] = target_features(target_ref[0].astype(f32))

        def write(cols, total):
            out_ref[0, :, cols] = total

        near_tile(held, left, right, write)


def source_specs(start, sides, rows, leaf):
    def spec(row):
        return pl.BlockSpec((1, rows, leaf), lambda i, table: (table[row, i + start], 0, 0))

    target = pl.BlockSpec((1, 16, leaf), lambda i, table: (table[BOX, i + start], 4, 0))
    return [spec((PREV, OWN, NEXT)[k]) for k in sides] + [target]


def tile_scratch(leaf):
    return [pltpu.VMEM((64, leaf), bf16), pltpu.VMEM((leaf, 32), bf16), pltpu.VMEM((32, leaf), bf16)]


def near_early(start, units, table, packed, halo=None):
    _, rows, leaf = packed.shape
    sides = (1,) if halo is None else (0, 1, 2)
    arrays = (packed,) if halo is None else (halo[0], packed, halo[1])
    return pl.pallas_call(
        functools.partial(early_kernel, start, sides),
        grid_spec=pltpu.PrefetchScalarGridSpec(
            num_scalar_prefetch=1,
            grid=(units,),
            in_specs=source_specs(start, sides, rows, leaf),
            out_specs=pl.BlockSpec((1, 64, leaf), lambda i, table: (i, 0, 0)),
            scratch_shapes=tile_scratch(leaf),
        ),
        out_shape=jax.ShapeDtypeStruct((units, 64, leaf), f32),
        compiler_params=params(40),
        cost_estimate=SMALL,
        name="near_early",
    )(table, *arrays, packed)


def last_kernel(sides, table, *refs):
    sources = refs[: len(sides)]
    target_ref, potential_ref, transfer_ref, down_ref, *refs = refs[len(sides) :]
    *early, out_ref, held, left, right, total_ref = refs
    column = pl.program_id(0) + LAST_AT
    box = table[BOX, column]

    @pl.when(table[OPENS, column] == 1)
    def _():
        total_ref[...] = jnp.zeros_like(total_ref)
        at = 0
        for ref in early:
            for k in range(ref.shape[0]):

                @pl.when((table[LIVE, at] == 1) & (table[BOX, at] == box))
                def _(ref=ref, k=k):
                    total_ref[...] += ref[k]

                at += 1

    @pl.when(table[LIVE, column] == 1)
    def _():
        load_source(table, column, list(zip(sides, sources)), held, left)
        right[...] = target_features(target_ref[0].astype(f32))

        def write(cols, total):
            total_ref[:, cols] += total

        near_tile(held, left, right, write)

    @pl.when(table[CLOSES, column] == 1)
    def _():
        box_potential = dot_nt(potential_ref[...], transfer_ref[0]).astype(bf16)
        out_ref[0] = (dot(box_potential, down_ref[0]) + total_ref[...] * LN2).astype(bf16)


def near_last(table, packed, halo, potential, box_transfer, down_basis, early):
    boxes, rows, leaf = packed.shape
    rank = down_basis.shape[1]
    sides = (0, 1, 2)

    def whole(shape):
        return pl.BlockSpec(shape, lambda i, table: (0,) * len(shape))

    def by_box(shape):
        return pl.BlockSpec(shape, lambda i, table: (table[BOX, i + LAST_AT], 0, 0))

    return pl.pallas_call(
        functools.partial(last_kernel, sides),
        grid_spec=pltpu.PrefetchScalarGridSpec(
            num_scalar_prefetch=1,
            grid=(LAST_UNITS,),
            in_specs=source_specs(LAST_AT, sides, rows, leaf)
            + [whole((64, rank)), by_box((1, rank, rank)), by_box((1, rank, leaf))]
            + [whole(part.shape) for part in early],
            out_specs=by_box((1, 64, leaf)),
            scratch_shapes=tile_scratch(leaf) + [pltpu.VMEM((64, leaf), f32)],
        ),
        out_shape=jax.ShapeDtypeStruct((boxes, 64, leaf), bf16),
        compiler_params=params(40),
        cost_estimate=SMALL,
        name="near_last",
    )(table, halo[0], packed, halo[1], packed, potential, box_transfer, down_basis, *early)


def group_kernel(skel_ref, nodes_ref, out_ref):
    nodes, _, rank = nodes_ref.shape
    total = jnp.zeros((64, rank), f32)
    found = jnp.zeros((16, rank), f32)
    skeleton = skel_ref[0]
    for k in range(nodes):
        total = total + nodes_ref[k, 80:144, :].astype(f32)
        found = found + dot(nodes_ref[k, 64:80, :], one_hot(skeleton, rank, k * rank))
    out_ref[...] = jnp.zeros_like(out_ref)
    out_ref[0:64, :] = total.astype(bf16)
    out_ref[64:80, :] = found.astype(bf16)


def group_pass(group_skeleton, tx_index, nodes):
    rank = nodes.shape[2]
    own = lax.dynamic_slice_in_dim(group_skeleton, tx_index, 1, 0)[None]
    return pl.pallas_call(
        group_kernel,
        in_specs=[VMEM] * 2,
        out_specs=VMEM,
        out_shape=jax.ShapeDtypeStruct((GROUP_ROWS, rank), bf16),
        compiler_params=params(),
        name="group_pass",
    )(own, nodes)


def far_kernel(place_ref, list_ref, nodes_ref, groups_ref, node_transfer_ref, out_ref):
    tx_index, ty_index = place_ref[0], place_ref[1]
    target = target_features(groups_ref[tx_index, 64:80, :].astype(f32))
    total = jnp.zeros(out_ref.shape, f32)
    for k in range(groups_ref.shape[0]):
        left = source_features(groups_ref[k, 64:80, :].astype(f32))
        term = dot(groups_ref[k, 0:64, :], entries(dot(left, target)))
        total = total + jnp.where(k != tx_index, term, 0.0)
    group_potential = (total * LN2).astype(bf16)
    target = target_features(nodes_ref[ty_index, 64:80, :].astype(f32))
    total = jnp.zeros(out_ref.shape, f32)
    for k in range(list_ref.shape[1]):
        slot = jnp.clip(list_ref[0, k] - tx_index * nodes_ref.shape[0], 0, nodes_ref.shape[0] - 1)
        left = source_features(nodes_ref[slot, 64:80, :].astype(f32))
        total = total + dot(nodes_ref[slot, 0:64, :], entries(dot(left, target)))
    out_ref[...] = (total * LN2 + dot_nt(group_potential, node_transfer_ref[0])).astype(bf16)


def far_pass(place, node_list, nodes, groups, node_transfer):
    rank = nodes.shape[2]
    return pl.pallas_call(
        far_kernel,
        in_specs=[SMEM] * 2 + [VMEM] * 3,
        out_specs=VMEM,
        out_shape=jax.ShapeDtypeStruct((64, rank), bf16),
        compiler_params=params(),
        cost_estimate=SMALL,
        name="far_pass",
    )(place, node_list, nodes, groups, node_transfer)


def shards(
    probes,
    points,
    up_basis,
    down_basis,
    box_skeleton,
    box_transfer,
    node_skeleton,
    node_transfer,
    group_skeleton,
    near_list,
    node_list,
):
    boxes = probes.shape[0]
    n_tx = lax.axis_size("tx")
    n_ty = lax.axis_size("ty")
    tx_index = lax.axis_index("tx")
    ty_index = lax.axis_index("ty")
    node = tx_index * n_ty + ty_index
    z_index, x_index = ty_index // 4, ty_index % 4
    base = ((node - 1) * boxes).astype(i32).reshape(1)

    packed, table = pack(near_list, base, probes, points)
    prev_box = lax.ppermute(packed, "ty", [(i, i + 1) for i in range(n_ty - 1)])
    next_box = lax.ppermute(packed, "ty", [(i + 1, i) for i in range(n_ty - 1)])

    own = up_pass(packed, up_basis, box_skeleton, box_transfer, node_skeleton, node_transfer)
    nodes = lax.all_gather(own, "ty", axis=0, tiled=False)
    halo = (prev_box, next_box)
    first = near_early(0, OWN_UNITS, table, packed)
    late_table, first = lax.optimization_barrier((table, first))
    second = near_early(OWN_UNITS, FIRST_LATE, late_table, packed, halo)
    second, nodes = lax.optimization_barrier((second, nodes))

    group = group_pass(group_skeleton, tx_index, nodes)
    third_table, group = lax.optimization_barrier((late_table, group))
    groups = lax.all_gather(group, "tx", axis=0, tiled=False)
    third = near_early(OWN_UNITS + FIRST_LATE, LATE_UNITS - FIRST_LATE, third_table, packed, halo)
    third, groups = lax.optimization_barrier((third, groups))

    place = jnp.stack([tx_index, ty_index]).astype(i32)
    potential = far_pass(place, node_list, nodes, groups, node_transfer)
    return near_last(table, packed, halo, potential, box_transfer, down_basis, (first, second, third))


def solution(mesh):
    spec3 = P(("tx", "ty"), None, None)
    spec2 = P(("tx", "ty"), None)
    in_specs = (spec3, spec3, spec3, spec3, spec2, spec3, spec2, spec3, P(), spec2, spec2)
    return jax.shard_map(shards, mesh=mesh, in_specs=in_specs, out_specs=spec3, check_vma=False)
```

```python
import functools
import math

import jax
import jax.numpy as jnp
from jax import lax
from jax.experimental import pallas as pl
from jax.experimental.pallas import tpu as pltpu
from jax.sharding import PartitionSpec as P

bf16 = jnp.bfloat16
f32 = jnp.float32
i32 = jnp.int32

INV_LENGTH = 4.0
LN2 = math.log(2.0)
SCALE = INV_LENGTH / LN2
VMEM = pl.BlockSpec(memory_space=pltpu.VMEM)
SMEM = pl.BlockSpec(memory_space=pltpu.SMEM)
TILE_ROWS = 1024
TILE_COLS = 256
OWN_UNITS = 4
LATE_UNITS = 7
FIRST_LATE = 3
GROUP_ROWS = 256
LAST_AT = OWN_UNITS + LATE_UNITS
LAST_UNITS = 7
COLUMNS = LAST_AT + LAST_UNITS
SIDE, BOX, LIVE, OPENS, CLOSES, PREV, OWN, NEXT = range(8)


def params(mib=62):
    return pltpu.CompilerParams(vmem_limit_bytes=mib * 2**20)


SMALL = pl.CostEstimate(flops=1024, bytes_accessed=1024, transcendentals=0)


def split_points(points):
    scaled = (points - 0.5) * SCALE
    high = scaled.astype(bf16)
    low = (scaled - high.astype(f32)).astype(bf16)
    return high, low


def norm_rows(pair, one_first):
    high = pair[:8]
    low = pair[8:]
    full = high + low
    norm = jnp.sum(full * full, axis=0, keepdims=True)
    first = norm.astype(bf16).astype(f32)
    rest = norm - first
    second = rest.astype(bf16).astype(f32)
    third = rest - second
    row = lax.broadcasted_iota(i32, high.shape, 0)
    base = 3 if one_first else 0
    ones = 0 if one_first else 3
    out = jnp.where((row >= ones) & (row < ones + 3), 1.0, 0.0)
    out = jnp.where(row == base, first, out)
    out = jnp.where(row == base + 1, second, out)
    return jnp.where(row == base + 2, third, out)


def source_features(pair):
    high = pair[:8] * -2.0
    low = pair[8:] * -2.0
    return jnp.concatenate([high, low, high, norm_rows(pair, False)], axis=0).T.astype(bf16)


def target_features(pair):
    high = pair[:8]
    return jnp.concatenate([high, high, pair[8:], norm_rows(pair, True)], axis=0).astype(bf16)


def entries(squared):
    squared = jnp.maximum(squared, 1e-12)
    scaled = squared * lax.rsqrt(squared)
    return (scaled * jnp.exp2(-scaled)).astype(bf16)


def dot(a, b):
    return jnp.dot(a, b, preferred_element_type=f32)


def dot_nt(a, b):
    return lax.dot_general(a, b, (((1,), (1,)), ((), ())), preferred_element_type=f32)


def write_table(near_ref, base_ref, table_ref):
    boxes, width = near_ref.shape
    for column in range(COLUMNS):
        table_ref[SIDE, column] = i32(1)
        table_ref[BOX, column] = i32(boxes - 1)
        for row in (LIVE, OPENS, CLOSES, PREV, OWN, NEXT):
            table_ref[row, column] = i32(0)

    units = []
    for box in range(boxes):
        for entry in range(width):
            named = near_ref[box, entry]
            slot = jnp.clip(named - base_ref[0], 0, 3 * boxes - 1)
            side = (slot >= boxes).astype(i32) + (slot >= 2 * boxes).astype(i32)
            units.append((box, named >= 0, side, slot - side * boxes))

    def put(column, when, box, side, index, hold):
        hold = [jnp.where(when & (side == k), index, hold[k]) for k in range(3)]

        @pl.when(when)
        def _():
            table_ref[SIDE, column] = side
            table_ref[BOX, column] = i32(box)
            table_ref[LIVE, column] = i32(1)
            for k, row in enumerate((PREV, OWN, NEXT)):
                table_ref[row, column] = hold[k]

        return hold

    zero = i32(0)
    own_rank = zero
    rest_rank = zero
    last_column = i32(LAST_AT)
    own_hold, late_hold, last_hold = [zero] * 3, [zero] * 3, [zero] * 3
    for box in range(boxes):
        opened = last_column
        for _, live, side, index in units[box * width : (box + 1) * width]:
            early = live & (side == 1) & (own_rank < OWN_UNITS)
            own_hold = put(own_rank, early, box, side, index, own_hold)
            own_rank = own_rank + early.astype(i32)
            rest = live & jnp.logical_not(early)
            late = rest & (rest_rank < LATE_UNITS)
            late_hold = put(OWN_UNITS + rest_rank, late, box, side, index, late_hold)
            rest_rank = rest_rank + rest.astype(i32)
            last = rest & jnp.logical_not(late)
            last_hold = put(last_column, last, box, side, index, last_hold)
            last_column = last_column + last.astype(i32)
        bare = last_column == opened

        @pl.when(bare)
        def _(column=last_column, box=box, hold=tuple(last_hold)):
            table_ref[BOX, column] = i32(box)
            for k, row in enumerate((PREV, OWN, NEXT)):
                table_ref[row, column] = hold[k]

        last_column = last_column + bare.astype(i32)
        table_ref[OPENS, opened] = i32(1)
        table_ref[CLOSES, last_column - 1] = i32(1)


def one_hot(index_row, size, offset=0):
    rows = lax.broadcasted_iota(i32, (size, index_row.shape[1]), 0) + offset
    return jnp.where(rows == index_row, 1.0, 0.0).astype(bf16)


def prep_kernel(
    near_ref,
    base_ref,
    probes_ref,
    points_ref,
    up_ref,
    box_skel_ref,
    transfer_ref,
    node_skel_ref,
    node_transfer_ref,
    packed_ref,
    table_ref,
    out_ref,
    acc,
    pool,
):
    b = pl.program_id(0)
    boxes = pl.num_programs(0)
    rank = up_ref.shape[1]
    leaf = up_ref.shape[2]

    @pl.when(b == 0)
    def _():
        write_table(near_ref, base_ref, table_ref)
        acc[...] = jnp.zeros_like(acc)

    packed_ref[0, :64, :] = probes_ref[0]
    high, low = split_points(points_ref[0])
    pair = jnp.concatenate([high.astype(f32), low.astype(f32)], axis=0).astype(bf16)
    packed_ref[0, 64:80, :] = pair
    weights = dot_nt(probes_ref[0], up_ref[0]).astype(bf16)
    acc[...] += dot(weights, transfer_ref[0])
    pool[b] = dot(pair, one_hot(box_skel_ref[pl.ds(b, 1), :], leaf)).astype(bf16)

    @pl.when(b == boxes - 1)
    def _():
        node_weight = acc[...].astype(bf16)
        out_ref[0:64, :] = node_weight
        found = jnp.zeros((16, rank), f32)
        for k in range(pool.shape[0]):
            found = found + dot(pool[k], one_hot(node_skel_ref[...], rank, k * rank))
        out_ref[64:80, :] = found.astype(bf16)
        out_ref[80:144, :] = dot(node_weight, node_transfer_ref[0]).astype(bf16)


def prep(near_list, base, probes, points, up_basis, box_skeleton, box_transfer, node_skeleton, node_transfer):
    boxes, count, leaf = probes.shape
    rank = up_basis.shape[1]

    def by_box(shape):
        return pl.BlockSpec((1,) + shape, lambda b: (b, 0, 0))

    def whole(shape):
        return pl.BlockSpec(shape, lambda b: (0,) * len(shape))

    return pl.pallas_call(
        prep_kernel,
        grid=(boxes,),
        in_specs=[
            SMEM,
            SMEM,
            by_box((count, leaf)),
            by_box((8, leaf)),
            by_box((rank, leaf)),
            whole((boxes, rank)),
            by_box((rank, rank)),
            whole((1, rank)),
            whole((1, rank, rank)),
        ],
        out_specs=[by_box((count + 16, leaf)), SMEM, whole((144, rank))],
        out_shape=[
            jax.ShapeDtypeStruct((boxes, count + 16, leaf), bf16),
            jax.ShapeDtypeStruct((8, COLUMNS), i32),
            jax.ShapeDtypeStruct((144, rank), bf16),
        ],
        scratch_shapes=[pltpu.VMEM((64, rank), f32), pltpu.VMEM((boxes, 16, rank), bf16)],
        compiler_params=params(),
        name="prep",
    )(near_list, base, probes, points, up_basis, box_skeleton, box_transfer, node_skeleton, node_transfer)


def load_source(table, column, sources, held, left):
    side = table[SIDE, column]
    for k, ref in sources:

        @pl.when(side == k)
        def _(ref=ref):
            held[...] = ref[0, :64, :]
            left[...] = source_features(ref[0, 64:80, :].astype(f32))


def near_tile(held, left, right, write):
    leaf = left.shape[0]
    steps = leaf // TILE_ROWS
    for j in range(leaf // TILE_COLS):
        cols = slice(j * TILE_COLS, (j + 1) * TILE_COLS)
        total = None
        block = None
        ahead = dot(left[0:TILE_ROWS, :], right[:, cols])
        for k in range(steps):
            squared = ahead
            if k + 1 < steps:
                ahead = dot(left[(k + 1) * TILE_ROWS : (k + 2) * TILE_ROWS, :], right[:, cols])
            before, block = block, entries(squared)
            if before is not None:
                term = dot(held[:, (k - 1) * TILE_ROWS : k * TILE_ROWS], before)
                total = term if total is None else total + term
        term = dot(held[:, (steps - 1) * TILE_ROWS :], block)
        write(cols, term if total is None else total + term)


def early_kernel(start, sides, table, *refs):
    sources = refs[: len(sides)]
    target_ref, out_ref, held, left, right = refs[len(sides) :]
    column = pl.program_id(0) + start

    @pl.when(table[LIVE, column] == 1)
    def _():
        load_source(table, column, list(zip(sides, sources)), held, left)
        right[...] = target_features(target_ref[0].astype(f32))

        def write(cols, total):
            out_ref[0, :, cols] = total

        near_tile(held, left, right, write)


def source_specs(start, sides, rows, leaf):
    def spec(row):
        return pl.BlockSpec((1, rows, leaf), lambda i, table: (table[row, i + start], 0, 0))

    target = pl.BlockSpec((1, 16, leaf), lambda i, table: (table[BOX, i + start], 4, 0))
    return [spec((PREV, OWN, NEXT)[k]) for k in sides] + [target]


def tile_scratch(leaf):
    return [pltpu.VMEM((64, leaf), bf16), pltpu.VMEM((leaf, 32), bf16), pltpu.VMEM((32, leaf), bf16)]


def near_early(start, units, table, packed, halo=None):
    _, rows, leaf = packed.shape
    sides = (1,) if halo is None else (0, 1, 2)
    arrays = (packed,) if halo is None else (halo[0], packed, halo[1])
    return pl.pallas_call(
        functools.partial(early_kernel, start, sides),
        grid_spec=pltpu.PrefetchScalarGridSpec(
            num_scalar_prefetch=1,
            grid=(units,),
            in_specs=source_specs(start, sides, rows, leaf),
            out_specs=pl.BlockSpec((1, 64, leaf), lambda i, table: (i, 0, 0)),
            scratch_shapes=tile_scratch(leaf),
        ),
        out_shape=jax.ShapeDtypeStruct((units, 64, leaf), f32),
        compiler_params=params(40),
        cost_estimate=SMALL,
        name="near_early",
    )(table, *arrays, packed)


def last_kernel(sides, table, *refs):
    sources = refs[: len(sides)]
    target_ref, potential_ref, transfer_ref, down_ref, *refs = refs[len(sides) :]
    *early, out_ref, held, left, right, total_ref = refs
    column = pl.program_id(0) + LAST_AT
    box = table[BOX, column]

    @pl.when(table[OPENS, column] == 1)
    def _():
        total_ref[...] = jnp.zeros_like(total_ref)
        at = 0
        for ref in early:
            for k in range(ref.shape[0]):

                @pl.when((table[LIVE, at] == 1) & (table[BOX, at] == box))
                def _(ref=ref, k=k):
                    total_ref[...] += ref[k]

                at += 1

    @pl.when(table[LIVE, column] == 1)
    def _():
        load_source(table, column, list(zip(sides, sources)), held, left)
        right[...] = target_features(target_ref[0].astype(f32))

        def write(cols, total):
            total_ref[:, cols] += total

        near_tile(held, left, right, write)

    @pl.when(table[CLOSES, column] == 1)
    def _():
        box_potential = dot_nt(potential_ref[...], transfer_ref[0]).astype(bf16)
        out_ref[0] = (dot(box_potential, down_ref[0]) + total_ref[...] * LN2).astype(bf16)


def near_last(table, packed, halo, potential, box_transfer, down_basis, early):
    boxes, rows, leaf = packed.shape
    rank = down_basis.shape[1]
    sides = (0, 1, 2)

    def whole(shape):
        return pl.BlockSpec(shape, lambda i, table: (0,) * len(shape))

    def by_box(shape):
        return pl.BlockSpec(shape, lambda i, table: (table[BOX, i + LAST_AT], 0, 0))

    return pl.pallas_call(
        functools.partial(last_kernel, sides),
        grid_spec=pltpu.PrefetchScalarGridSpec(
            num_scalar_prefetch=1,
            grid=(LAST_UNITS,),
            in_specs=source_specs(LAST_AT, sides, rows, leaf)
            + [whole((64, rank)), by_box((1, rank, rank)), by_box((1, rank, leaf))]
            + [pl.BlockSpec(part.shape, lambda i, table: (0, 0, 0), pipeline_mode=pl.Buffered(1)) for part in early],
            out_specs=by_box((1, 64, leaf)),
            scratch_shapes=tile_scratch(leaf) + [pltpu.VMEM((64, leaf), f32)],
        ),
        out_shape=jax.ShapeDtypeStruct((boxes, 64, leaf), bf16),
        compiler_params=params(40),
        cost_estimate=SMALL,
        name="near_last",
    )(table, halo[0], packed, halo[1], packed, potential, box_transfer, down_basis, *early)


def group_kernel(place_ref, skel_ref, nodes_ref, out_ref):
    nodes, _, rank = nodes_ref.shape
    total = jnp.zeros((64, rank), f32)
    found = jnp.zeros((16, rank), f32)
    skeleton = skel_ref[pl.ds(place_ref[0], 1), :]
    for k in range(nodes):
        total = total + nodes_ref[k, 80:144, :].astype(f32)
        found = found + dot(nodes_ref[k, 64:80, :], one_hot(skeleton, rank, k * rank))
    out_ref[...] = jnp.zeros_like(out_ref)
    out_ref[0:64, :] = total.astype(bf16)
    out_ref[64:80, :] = found.astype(bf16)


def group_pass(place, group_skeleton, nodes):
    rank = nodes.shape[2]
    return pl.pallas_call(
        group_kernel,
        in_specs=[SMEM] + [VMEM] * 2,
        out_specs=VMEM,
        out_shape=jax.ShapeDtypeStruct((GROUP_ROWS, rank), bf16),
        compiler_params=params(16),
        name="group_pass",
    )(place, group_skeleton, nodes)


def far_kernel(group_at_ref, node_at_ref, list_ref, nodes_ref, groups_ref, node_transfer_ref, out_ref):
    tx_index, ty_index = group_at_ref[0], node_at_ref[0]
    target = target_features(groups_ref[tx_index, 64:80, :].astype(f32))
    total = jnp.zeros(out_ref.shape, f32)
    for k in range(groups_ref.shape[0]):
        left = source_features(groups_ref[k, 64:80, :].astype(f32))
        term = dot(groups_ref[k, 0:64, :], entries(dot(left, target)))
        total = total + jnp.where(k != tx_index, term, 0.0)
    group_potential = (total * LN2).astype(bf16)
    target = target_features(nodes_ref[ty_index, 64:80, :].astype(f32))
    total = jnp.zeros(out_ref.shape, f32)
    for k in range(list_ref.shape[1]):
        slot = jnp.clip(list_ref[0, k] - tx_index * nodes_ref.shape[0], 0, nodes_ref.shape[0] - 1)
        left = source_features(nodes_ref[slot, 64:80, :].astype(f32))
        total = total + dot(nodes_ref[slot, 0:64, :], entries(dot(left, target)))
    out_ref[...] = (total * LN2 + dot_nt(group_potential, node_transfer_ref[0])).astype(bf16)


def far_pass(group_at, node_at, node_list, nodes, groups, node_transfer):
    rank = nodes.shape[2]
    return pl.pallas_call(
        far_kernel,
        in_specs=[SMEM] * 3 + [VMEM] * 3,
        out_specs=VMEM,
        out_shape=jax.ShapeDtypeStruct((64, rank), bf16),
        compiler_params=params(16),
        cost_estimate=SMALL,
        name="far_pass",
    )(group_at, node_at, node_list, nodes, groups, node_transfer)


def shards(
    probes,
    points,
    up_basis,
    down_basis,
    box_skeleton,
    box_transfer,
    node_skeleton,
    node_transfer,
    group_skeleton,
    near_list,
    node_list,
):
    boxes = probes.shape[0]
    n_tx = lax.axis_size("tx")
    n_ty = lax.axis_size("ty")
    tx_index = lax.axis_index("tx")
    ty_index = lax.axis_index("ty")
    node = tx_index * n_ty + ty_index
    base = ((node - 1) * boxes).astype(i32).reshape(1)

    group_at = tx_index.astype(i32).reshape(1)
    node_at = ty_index.astype(i32).reshape(1)
    packed, table, own = prep(
        near_list, base, probes, points, up_basis, box_skeleton, box_transfer, node_skeleton, node_transfer
    )
    prev_box = lax.ppermute(packed, "ty", [(i, i + 1) for i in range(n_ty - 1)])
    next_box = lax.ppermute(packed, "ty", [(i + 1, i) for i in range(n_ty - 1)])
    nodes = lax.all_gather(own, "ty", axis=0, tiled=False)
    halo = (prev_box, next_box)
    first = near_early(0, OWN_UNITS, table, packed)
    late_table, first = lax.optimization_barrier((table, first))
    second = near_early(OWN_UNITS, FIRST_LATE, late_table, packed, halo)
    second, nodes = lax.optimization_barrier((second, nodes))

    group = group_pass(group_at, group_skeleton, nodes)
    third_table, group = lax.optimization_barrier((late_table, group))
    groups = lax.all_gather(group, "tx", axis=0, tiled=False)
    third = near_early(OWN_UNITS + FIRST_LATE, LATE_UNITS - FIRST_LATE, third_table, packed, halo)
    third, groups = lax.optimization_barrier((third, groups))

    potential = far_pass(group_at, node_at, node_list, nodes, groups, node_transfer)
    return near_last(table, packed, halo, potential, box_transfer, down_basis, (first, second, third))


def solution(mesh):
    spec3 = P(("tx", "ty"), None, None)
    spec2 = P(("tx", "ty"), None)
    in_specs = (spec3, spec3, spec3, spec3, spec2, spec3, spec2, spec3, P(), spec2, spec2)
    return jax.shard_map(shards, mesh=mesh, in_specs=in_specs, out_specs=spec3, check_vma=False)
```

```python
import functools
import math

import jax
import jax.numpy as jnp
from jax import lax
from jax.experimental import pallas as pl
from jax.experimental.pallas import tpu as pltpu
from jax.sharding import PartitionSpec as P

bf16 = jnp.bfloat16
f32 = jnp.float32
i32 = jnp.int32

INV_LENGTH = 4.0
LN2 = math.log(2.0)
SCALE = INV_LENGTH / LN2
VMEM = pl.BlockSpec(memory_space=pltpu.VMEM)
SMEM = pl.BlockSpec(memory_space=pltpu.SMEM)
TILE_ROWS = 512
TILE_COLS = 256
OWN_UNITS = 4
LATE_UNITS = 8
FIRST_LATE = 3
GROUP_ROWS = 256
LAST_AT = OWN_UNITS + LATE_UNITS
LAST_UNITS = 6
COLUMNS = LAST_AT + LAST_UNITS
SIDE, BOX, LIVE, OPENS, CLOSES, PREV, OWN, NEXT = range(8)


def params(mib=62):
    return pltpu.CompilerParams(vmem_limit_bytes=mib * 2**20)


SMALL = pl.CostEstimate(flops=1024, bytes_accessed=1024, transcendentals=0)


def split_points(points):
    scaled = (points - 0.5) * SCALE
    high = scaled.astype(bf16)
    low = (scaled - high.astype(f32)).astype(bf16)
    return high, low


def norm_rows(pair, one_first):
    high = pair[:8]
    low = pair[8:]
    full = high + low
    norm = jnp.sum(full * full, axis=0, keepdims=True)
    first = norm.astype(bf16).astype(f32)
    rest = norm - first
    second = rest.astype(bf16).astype(f32)
    third = rest - second
    row = lax.broadcasted_iota(i32, high.shape, 0)
    base = 3 if one_first else 0
    ones = 0 if one_first else 3
    out = jnp.where((row >= ones) & (row < ones + 3), 1.0, 0.0)
    out = jnp.where(row == base, first, out)
    out = jnp.where(row == base + 1, second, out)
    return jnp.where(row == base + 2, third, out)


def source_features(pair):
    high = pair[:8] * -2.0
    low = pair[8:] * -2.0
    return jnp.concatenate([high, low, high, norm_rows(pair, False)], axis=0).T.astype(bf16)


def target_features(pair):
    high = pair[:8]
    return jnp.concatenate([high, high, pair[8:], norm_rows(pair, True)], axis=0).astype(bf16)


def entries(squared):
    squared = jnp.maximum(squared, 1e-12)
    scaled = squared * lax.rsqrt(squared)
    return (scaled * jnp.exp2(-scaled)).astype(bf16)


def dot(a, b):
    return jnp.dot(a, b, preferred_element_type=f32)


def dot_nt(a, b):
    return lax.dot_general(a, b, (((1,), (1,)), ((), ())), preferred_element_type=f32)


def write_table(near_ref, base_ref, table_ref):
    boxes, width = near_ref.shape
    for column in range(COLUMNS):
        table_ref[SIDE, column] = i32(1)
        table_ref[BOX, column] = i32(boxes - 1)
        for row in (LIVE, OPENS, CLOSES, PREV, OWN, NEXT):
            table_ref[row, column] = i32(0)

    units = []
    for box in range(boxes):
        for entry in range(width):
            named = near_ref[box, entry]
            slot = jnp.clip(named - base_ref[0], 0, 3 * boxes - 1)
            side = (slot >= boxes).astype(i32) + (slot >= 2 * boxes).astype(i32)
            units.append((box, named >= 0, side, slot - side * boxes))

    def put(column, when, box, side, index, hold):
        hold = [jnp.where(when & (side == k), index, hold[k]) for k in range(3)]

        @pl.when(when)
        def _():
            table_ref[SIDE, column] = side
            table_ref[BOX, column] = i32(box)
            table_ref[LIVE, column] = i32(1)
            for k, row in enumerate((PREV, OWN, NEXT)):
                table_ref[row, column] = hold[k]

        return hold

    zero = i32(0)
    own_rank = zero
    rest_rank = zero
    last_column = i32(LAST_AT)
    own_hold, late_hold, last_hold = [zero] * 3, [zero] * 3, [zero] * 3
    for box in range(boxes):
        opened = last_column
        for _, live, side, index in units[box * width : (box + 1) * width]:
            early = live & (side == 1) & (own_rank < OWN_UNITS)
            own_hold = put(own_rank, early, box, side, index, own_hold)
            own_rank = own_rank + early.astype(i32)
            rest = live & jnp.logical_not(early)
            late = rest & (rest_rank < LATE_UNITS)
            late_hold = put(OWN_UNITS + rest_rank, late, box, side, index, late_hold)
            rest_rank = rest_rank + rest.astype(i32)
            last = rest & jnp.logical_not(late)
            last_hold = put(last_column, last, box, side, index, last_hold)
            last_column = last_column + last.astype(i32)
        bare = last_column == opened

        @pl.when(bare)
        def _(column=last_column, box=box, hold=tuple(last_hold)):
            table_ref[BOX, column] = i32(box)
            for k, row in enumerate((PREV, OWN, NEXT)):
                table_ref[row, column] = hold[k]

        last_column = last_column + bare.astype(i32)
        table_ref[OPENS, opened] = i32(1)
        table_ref[CLOSES, last_column - 1] = i32(1)


def one_hot(index_row, size, offset=0):
    rows = lax.broadcasted_iota(i32, (size, index_row.shape[1]), 0) + offset
    return jnp.where(rows == index_row, 1.0, 0.0).astype(bf16)


def prep_kernel(
    near_ref,
    base_ref,
    probes_ref,
    points_ref,
    up_ref,
    box_skel_ref,
    transfer_ref,
    node_skel_ref,
    node_transfer_ref,
    packed_ref,
    table_ref,
    out_ref,
    acc,
    pool,
):
    b = pl.program_id(0)
    boxes = pl.num_programs(0)
    rank = up_ref.shape[1]
    leaf = up_ref.shape[2]

    @pl.when(b == 0)
    def _():
        write_table(near_ref, base_ref, table_ref)
        acc[...] = jnp.zeros_like(acc)

    packed_ref[0, :64, :] = probes_ref[0]
    high, low = split_points(points_ref[0])
    pair = jnp.concatenate([high.astype(f32), low.astype(f32)], axis=0).astype(bf16)
    packed_ref[0, 64:80, :] = pair
    weights = dot_nt(probes_ref[0], up_ref[0]).astype(bf16)
    acc[...] += dot(weights, transfer_ref[0])
    pool[b] = dot(pair, one_hot(box_skel_ref[pl.ds(b, 1), :], leaf)).astype(bf16)

    @pl.when(b == boxes - 1)
    def _():
        node_weight = acc[...].astype(bf16)
        out_ref[0:64, :] = node_weight
        found = jnp.zeros((16, rank), f32)
        for k in range(pool.shape[0]):
            found = found + dot(pool[k], one_hot(node_skel_ref[...], rank, k * rank))
        out_ref[64:80, :] = found.astype(bf16)
        out_ref[80:144, :] = dot(node_weight, node_transfer_ref[0]).astype(bf16)


def prep(near_list, base, probes, points, up_basis, box_skeleton, box_transfer, node_skeleton, node_transfer):
    boxes, count, leaf = probes.shape
    rank = up_basis.shape[1]

    def by_box(shape):
        return pl.BlockSpec((1,) + shape, lambda b: (b, 0, 0))

    def whole(shape):
        return pl.BlockSpec(shape, lambda b: (0,) * len(shape))

    return pl.pallas_call(
        prep_kernel,
        grid=(boxes,),
        in_specs=[
            SMEM,
            SMEM,
            by_box((count, leaf)),
            by_box((8, leaf)),
            by_box((rank, leaf)),
            whole((boxes, rank)),
            by_box((rank, rank)),
            whole((1, rank)),
            whole((1, rank, rank)),
        ],
        out_specs=[by_box((count + 16, leaf)), SMEM, whole((144, rank))],
        out_shape=[
            jax.ShapeDtypeStruct((boxes, count + 16, leaf), bf16),
            jax.ShapeDtypeStruct((8, COLUMNS), i32),
            jax.ShapeDtypeStruct((144, rank), bf16),
        ],
        scratch_shapes=[pltpu.VMEM((64, rank), f32), pltpu.VMEM((boxes, 16, rank), bf16)],
        compiler_params=params(),
        name="prep",
    )(near_list, base, probes, points, up_basis, box_skeleton, box_transfer, node_skeleton, node_transfer)


def load_source(table, column, sources, held, left):
    side = table[SIDE, column]
    for k, ref in sources:

        @pl.when(side == k)
        def _(ref=ref):
            held[...] = ref[0, :64, :]
            left[...] = source_features(ref[0, 64:80, :].astype(f32))


def near_tile(held, left, right, write):
    leaf = left.shape[0]
    steps = leaf // TILE_ROWS
    for j in range(leaf // TILE_COLS):
        cols = slice(j * TILE_COLS, (j + 1) * TILE_COLS)
        total = None
        block = None
        ahead = dot(left[0:TILE_ROWS, :], right[:, cols])
        for k in range(steps):
            squared = ahead
            if k + 1 < steps:
                ahead = dot(left[(k + 1) * TILE_ROWS : (k + 2) * TILE_ROWS, :], right[:, cols])
            before, block = block, entries(squared)
            if before is not None:
                term = dot(held[:, (k - 1) * TILE_ROWS : k * TILE_ROWS], before)
                total = term if total is None else total + term
        term = dot(held[:, (steps - 1) * TILE_ROWS :], block)
        write(cols, term if total is None else total + term)


def early_kernel(start, sides, table, *refs):
    sources = refs[: len(sides)]
    target_ref, out_ref, held, left, right = refs[len(sides) :]
    column = pl.program_id(0) + start

    @pl.when(table[LIVE, column] == 1)
    def _():
        load_source(table, column, list(zip(sides, sources)), held, left)
        right[...] = target_features(target_ref[0].astype(f32))

        def write(cols, total):
            out_ref[0, :, cols] = total

        near_tile(held, left, right, write)


def source_specs(start, sides, rows, leaf):
    def spec(row):
        return pl.BlockSpec((1, rows, leaf), lambda i, table: (table[row, i + start], 0, 0))

    target = pl.BlockSpec((1, 16, leaf), lambda i, table: (table[BOX, i + start], 4, 0))
    return [spec((PREV, OWN, NEXT)[k]) for k in sides] + [target]


def tile_scratch(leaf):
    return [pltpu.VMEM((64, leaf), bf16), pltpu.VMEM((leaf, 32), bf16), pltpu.VMEM((32, leaf), bf16)]


def near_early(start, units, table, packed, halo=None):
    _, rows, leaf = packed.shape
    sides = (1,) if halo is None else (0, 1, 2)
    arrays = (packed,) if halo is None else (halo[0], packed, halo[1])
    return pl.pallas_call(
        functools.partial(early_kernel, start, sides),
        grid_spec=pltpu.PrefetchScalarGridSpec(
            num_scalar_prefetch=1,
            grid=(units,),
            in_specs=source_specs(start, sides, rows, leaf),
            out_specs=pl.BlockSpec((1, 64, leaf), lambda i, table: (i, 0, 0)),
            scratch_shapes=tile_scratch(leaf),
        ),
        out_shape=jax.ShapeDtypeStruct((units, 64, leaf), f32),
        compiler_params=params(),
        cost_estimate=SMALL,
        name="near_early",
    )(table, *arrays, packed)


def last_kernel(sides, table, *refs):
    sources = refs[: len(sides)]
    target_ref, potential_ref, transfer_ref, down_ref, *refs = refs[len(sides) :]
    *early, out_ref, held, left, right, total_ref = refs
    column = pl.program_id(0) + LAST_AT
    box = table[BOX, column]

    @pl.when(table[OPENS, column] == 1)
    def _():
        total_ref[...] = jnp.zeros_like(total_ref)
        at = 0
        for ref in early:
            for k in range(ref.shape[0]):

                @pl.when((table[LIVE, at] == 1) & (table[BOX, at] == box))
                def _(ref=ref, k=k):
                    total_ref[...] += ref[k]

                at += 1

    @pl.when(table[LIVE, column] == 1)
    def _():
        load_source(table, column, list(zip(sides, sources)), held, left)
        right[...] = target_features(target_ref[0].astype(f32))

        def write(cols, total):
            total_ref[:, cols] += total

        near_tile(held, left, right, write)

    @pl.when(table[CLOSES, column] == 1)
    def _():
        box_potential = dot_nt(potential_ref[...], transfer_ref[0]).astype(bf16)
        out_ref[0] = (dot(box_potential, down_ref[0]) + total_ref[...] * LN2).astype(bf16)


def near_last(table, packed, halo, potential, box_transfer, down_basis, early):
    boxes, rows, leaf = packed.shape
    rank = down_basis.shape[1]
    sides = (0, 1, 2)

    def whole(shape):
        return pl.BlockSpec(shape, lambda i, table: (0,) * len(shape))

    def by_box(shape):
        return pl.BlockSpec(shape, lambda i, table: (table[BOX, i + LAST_AT], 0, 0))

    return pl.pallas_call(
        functools.partial(last_kernel, sides),
        grid_spec=pltpu.PrefetchScalarGridSpec(
            num_scalar_prefetch=1,
            grid=(LAST_UNITS,),
            in_specs=source_specs(LAST_AT, sides, rows, leaf)
            + [whole((64, rank)), by_box((1, rank, rank)), by_box((1, rank, leaf))]
            + [pl.BlockSpec(part.shape, lambda i, table: (0, 0, 0), pipeline_mode=pl.Buffered(1)) for part in early],
            out_specs=by_box((1, 64, leaf)),
            scratch_shapes=tile_scratch(leaf) + [pltpu.VMEM((64, leaf), f32)],
        ),
        out_shape=jax.ShapeDtypeStruct((boxes, 64, leaf), bf16),
        compiler_params=params(),
        cost_estimate=SMALL,
        name="near_last",
    )(table, halo[0], packed, halo[1], packed, potential, box_transfer, down_basis, *early)


def group_kernel(place_ref, skel_ref, nodes_ref, out_ref):
    nodes, _, rank = nodes_ref.shape
    total = jnp.zeros((64, rank), f32)
    found = jnp.zeros((16, rank), f32)
    skeleton = skel_ref[pl.ds(place_ref[0], 1), :]
    for k in range(nodes):
        total = total + nodes_ref[k, 80:144, :].astype(f32)
        found = found + dot(nodes_ref[k, 64:80, :], one_hot(skeleton, rank, k * rank))
    out_ref[...] = jnp.zeros_like(out_ref)
    out_ref[0:64, :] = total.astype(bf16)
    out_ref[64:80, :] = found.astype(bf16)


def group_pass(place, group_skeleton, nodes):
    rank = nodes.shape[2]
    return pl.pallas_call(
        group_kernel,
        in_specs=[SMEM] + [VMEM] * 2,
        out_specs=VMEM,
        out_shape=jax.ShapeDtypeStruct((GROUP_ROWS, rank), bf16),
        compiler_params=params(),
        name="group_pass",
    )(place, group_skeleton, nodes)


def far_kernel(group_at_ref, node_at_ref, list_ref, nodes_ref, groups_ref, node_transfer_ref, out_ref):
    tx_index, ty_index = group_at_ref[0], node_at_ref[0]
    target = target_features(groups_ref[tx_index, 64:80, :].astype(f32))
    total = jnp.zeros(out_ref.shape, f32)
    for k in range(groups_ref.shape[0]):
        left = source_features(groups_ref[k, 64:80, :].astype(f32))
        term = dot(groups_ref[k, 0:64, :], entries(dot(left, target)))
        total = total + jnp.where(k != tx_index, term, 0.0)
    group_potential = (total * LN2).astype(bf16)
    target = target_features(nodes_ref[ty_index, 64:80, :].astype(f32))
    total = jnp.zeros(out_ref.shape, f32)
    for k in range(list_ref.shape[1]):
        slot = jnp.clip(list_ref[0, k] - tx_index * nodes_ref.shape[0], 0, nodes_ref.shape[0] - 1)
        left = source_features(nodes_ref[slot, 64:80, :].astype(f32))
        total = total + dot(nodes_ref[slot, 0:64, :], entries(dot(left, target)))
    out_ref[...] = (total * LN2 + dot_nt(group_potential, node_transfer_ref[0])).astype(bf16)


def far_pass(group_at, node_at, node_list, nodes, groups, node_transfer):
    rank = nodes.shape[2]
    return pl.pallas_call(
        far_kernel,
        in_specs=[SMEM] * 3 + [VMEM] * 3,
        out_specs=VMEM,
        out_shape=jax.ShapeDtypeStruct((64, rank), bf16),
        compiler_params=params(),
        cost_estimate=SMALL,
        name="far_pass",
    )(group_at, node_at, node_list, nodes, groups, node_transfer)


def shards(
    probes,
    points,
    up_basis,
    down_basis,
    box_skeleton,
    box_transfer,
    node_skeleton,
    node_transfer,
    group_skeleton,
    near_list,
    node_list,
):
    boxes = probes.shape[0]
    n_tx = lax.axis_size("tx")
    n_ty = lax.axis_size("ty")
    tx_index = lax.axis_index("tx")
    ty_index = lax.axis_index("ty")
    node = tx_index * n_ty + ty_index
    base = ((node - 1) * boxes).astype(i32).reshape(1)

    group_at = tx_index.astype(i32).reshape(1)
    node_at = ty_index.astype(i32).reshape(1)
    packed, table, own = prep(
        near_list, base, probes, points, up_basis, box_skeleton, box_transfer, node_skeleton, node_transfer
    )
    prev_box = lax.ppermute(packed, "ty", [(i, i + 1) for i in range(n_ty - 1)])
    next_box = lax.ppermute(packed, "ty", [(i + 1, i) for i in range(n_ty - 1)])
    nodes = lax.all_gather(own, "ty", axis=0, tiled=False)
    halo = (prev_box, next_box)
    first = near_early(0, OWN_UNITS, table, packed)
    late_table, first = lax.optimization_barrier((table, first))
    second = near_early(OWN_UNITS, FIRST_LATE, late_table, packed, halo)
    second, nodes = lax.optimization_barrier((second, nodes))

    group = group_pass(group_at, group_skeleton, nodes)
    third_table, group = lax.optimization_barrier((late_table, group))
    groups = lax.all_gather(group, "tx", axis=0, tiled=False)
    third = near_early(OWN_UNITS + FIRST_LATE, LATE_UNITS - FIRST_LATE, third_table, packed, halo)
    third, groups = lax.optimization_barrier((third, groups))

    potential = far_pass(group_at, node_at, node_list, nodes, groups, node_transfer)
    return near_last(table, packed, halo, potential, box_transfer, down_basis, (first, second, third))


def solution(mesh):
    spec3 = P(("tx", "ty"), None, None)
    spec2 = P(("tx", "ty"), None)
    in_specs = (spec3, spec3, spec3, spec3, spec2, spec3, spec2, spec3, P(), spec2, spec2)
    return jax.shard_map(shards, mesh=mesh, in_specs=in_specs, out_specs=spec3, check_vma=False)
```

```python
import functools
import math

import jax
import jax.numpy as jnp
from jax import lax
from jax.experimental import pallas as pl
from jax.experimental.pallas import tpu as pltpu
from jax.sharding import PartitionSpec as P

bf16 = jnp.bfloat16
f32 = jnp.float32
i32 = jnp.int32

INV_LENGTH = 4.0
LN2 = math.log(2.0)
SCALE = INV_LENGTH / LN2
VMEM = pl.BlockSpec(memory_space=pltpu.VMEM)
SMEM = pl.BlockSpec(memory_space=pltpu.SMEM)
TILE_ROWS = 512
TILE_COLS = 256
OWN_UNITS = 4
LATE_UNITS = 4
GROUP_ROWS = 256
LAST_AT = OWN_UNITS + LATE_UNITS
LAST_UNITS = 9
COLUMNS = LAST_AT + LAST_UNITS
SIDE, BOX, LIVE, OPENS, CLOSES, PREV, OWN, NEXT = range(8)


def params(mib=62):
    return pltpu.CompilerParams(vmem_limit_bytes=mib * 2**20)


SMALL = pl.CostEstimate(flops=1024, bytes_accessed=1024, transcendentals=0)
LARGE = pl.CostEstimate(flops=2**40, bytes_accessed=2**28, transcendentals=0)


def split_points(points):
    scaled = (points - 0.5) * SCALE
    high = scaled.astype(bf16)
    low = (scaled - high.astype(f32)).astype(bf16)
    return high, low


def norm_rows(pair, one_first):
    high = pair[:8]
    low = pair[8:]
    full = high + low
    norm = jnp.sum(full * full, axis=0, keepdims=True)
    first = norm.astype(bf16).astype(f32)
    rest = norm - first
    second = rest.astype(bf16).astype(f32)
    third = rest - second
    row = lax.broadcasted_iota(i32, high.shape, 0)
    base = 3 if one_first else 0
    ones = 0 if one_first else 3
    out = jnp.where((row >= ones) & (row < ones + 3), 1.0, 0.0)
    out = jnp.where(row == base, first, out)
    out = jnp.where(row == base + 1, second, out)
    return jnp.where(row == base + 2, third, out)


def source_features(pair):
    high = pair[:8] * -2.0
    low = pair[8:] * -2.0
    return jnp.concatenate([high, low, high, norm_rows(pair, False)], axis=0).T.astype(bf16)


def target_features(pair):
    high = pair[:8]
    return jnp.concatenate([high, high, pair[8:], norm_rows(pair, True)], axis=0).astype(bf16)


def entries(squared):
    squared = jnp.maximum(squared, 1e-12)
    scaled = squared * lax.rsqrt(squared)
    return (scaled * jnp.exp2(-scaled)).astype(bf16)


def dot(a, b):
    return jnp.dot(a, b, preferred_element_type=f32)


def dot_nt(a, b):
    return lax.dot_general(a, b, (((1,), (1,)), ((), ())), preferred_element_type=f32)


def write_table(near_ref, base_ref, table_ref):
    boxes, width = near_ref.shape
    for column in range(COLUMNS):
        table_ref[SIDE, column] = i32(1)
        table_ref[BOX, column] = i32(boxes - 1)
        for row in (LIVE, OPENS, CLOSES, PREV, OWN, NEXT):
            table_ref[row, column] = i32(0)

    units = []
    for box in range(boxes):
        for entry in range(width):
            named = near_ref[box, entry]
            slot = jnp.clip(named - base_ref[0], 0, 3 * boxes - 1)
            side = (slot >= boxes).astype(i32) + (slot >= 2 * boxes).astype(i32)
            units.append((box, named >= 0, side, slot - side * boxes))

    def put(column, when, box, side, index, hold):
        hold = [jnp.where(when & (side == k), index, hold[k]) for k in range(3)]

        @pl.when(when)
        def _():
            table_ref[SIDE, column] = side
            table_ref[BOX, column] = i32(box)
            table_ref[LIVE, column] = i32(1)
            for k, row in enumerate((PREV, OWN, NEXT)):
                table_ref[row, column] = hold[k]

        return hold

    zero = i32(0)
    own_rank = zero
    rest_rank = zero
    last_column = i32(LAST_AT)
    own_hold, late_hold, last_hold = [zero] * 3, [zero] * 3, [zero] * 3
    for box in range(boxes):
        opened = last_column
        for _, live, side, index in units[box * width : (box + 1) * width]:
            early = live & (side == 1) & (own_rank < OWN_UNITS)
            own_hold = put(own_rank, early, box, side, index, own_hold)
            own_rank = own_rank + early.astype(i32)
            rest = live & jnp.logical_not(early)
            late = rest & (rest_rank < LATE_UNITS)
            late_hold = put(OWN_UNITS + rest_rank, late, box, side, index, late_hold)
            rest_rank = rest_rank + rest.astype(i32)
            last = rest & jnp.logical_not(late)
            last_hold = put(last_column, last, box, side, index, last_hold)
            last_column = last_column + last.astype(i32)
        bare = last_column == opened

        @pl.when(bare)
        def _(column=last_column, box=box, hold=tuple(last_hold)):
            table_ref[BOX, column] = i32(box)
            for k, row in enumerate((PREV, OWN, NEXT)):
                table_ref[row, column] = hold[k]

        last_column = last_column + bare.astype(i32)
        table_ref[OPENS, opened] = i32(1)
        table_ref[CLOSES, last_column - 1] = i32(1)


def one_hot(index_row, size, offset=0):
    rows = lax.broadcasted_iota(i32, (size, index_row.shape[1]), 0) + offset
    return jnp.where(rows == index_row, 1.0, 0.0).astype(bf16)


def prep_kernel(
    near_ref,
    base_ref,
    probes_ref,
    points_ref,
    up_ref,
    box_skel_ref,
    transfer_ref,
    node_skel_ref,
    node_transfer_ref,
    pair_ref,
    table_ref,
    out_ref,
    acc,
    pool,
):
    b = pl.program_id(0)
    boxes = pl.num_programs(0)
    rank = up_ref.shape[1]
    leaf = up_ref.shape[2]

    @pl.when(b == 0)
    def _():
        write_table(near_ref, base_ref, table_ref)
        acc[...] = jnp.zeros_like(acc)

    high, low = split_points(points_ref[0])
    pair = jnp.concatenate([high.astype(f32), low.astype(f32)], axis=0).astype(bf16)
    pair_ref[0] = pair
    weights = dot_nt(probes_ref[0], up_ref[0]).astype(bf16)
    acc[...] += dot(weights, transfer_ref[0])
    pool[b] = dot(pair, one_hot(box_skel_ref[pl.ds(b, 1), :], leaf)).astype(bf16)

    @pl.when(b == boxes - 1)
    def _():
        node_weight = acc[...].astype(bf16)
        out_ref[0:64, :] = node_weight
        found = jnp.zeros((16, rank), f32)
        for k in range(pool.shape[0]):
            found = found + dot(pool[k], one_hot(node_skel_ref[...], rank, k * rank))
        out_ref[64:80, :] = found.astype(bf16)
        out_ref[80:144, :] = dot(node_weight, node_transfer_ref[0]).astype(bf16)


def prep(near_list, base, probes, points, up_basis, box_skeleton, box_transfer, node_skeleton, node_transfer):
    boxes, count, leaf = probes.shape
    rank = up_basis.shape[1]

    def by_box(shape):
        return pl.BlockSpec((1,) + shape, lambda b: (b, 0, 0))

    def whole(shape):
        return pl.BlockSpec(shape, lambda b: (0,) * len(shape))

    return pl.pallas_call(
        prep_kernel,
        grid=(boxes,),
        in_specs=[
            SMEM,
            SMEM,
            by_box((count, leaf)),
            by_box((8, leaf)),
            by_box((rank, leaf)),
            whole((boxes, rank)),
            by_box((rank, rank)),
            whole((1, rank)),
            whole((1, rank, rank)),
        ],
        out_specs=[by_box((16, leaf)), SMEM, whole((144, rank))],
        out_shape=[
            jax.ShapeDtypeStruct((boxes, 16, leaf), bf16),
            jax.ShapeDtypeStruct((8, COLUMNS), i32),
            jax.ShapeDtypeStruct((144, rank), bf16),
        ],
        scratch_shapes=[pltpu.VMEM((64, rank), f32), pltpu.VMEM((boxes, 16, rank), bf16)],
        compiler_params=params(),
        name="prep",
    )(near_list, base, probes, points, up_basis, box_skeleton, box_transfer, node_skeleton, node_transfer)


def load_source(table, column, sources, held, left):
    side = table[SIDE, column]
    for k, probes_ref, pair_ref in sources:

        @pl.when(side == k)
        def _(probes_ref=probes_ref, pair_ref=pair_ref):
            held[...] = probes_ref[0]
            left[...] = source_features(pair_ref[0].astype(f32))


def near_tile(held, left, right, write):
    leaf = left.shape[0]
    steps = leaf // TILE_ROWS
    for j in range(leaf // TILE_COLS):
        cols = slice(j * TILE_COLS, (j + 1) * TILE_COLS)
        total = None
        block = None
        ahead = dot(left[0:TILE_ROWS, :], right[:, cols])
        for k in range(steps):
            squared = ahead
            if k + 1 < steps:
                ahead = dot(left[(k + 1) * TILE_ROWS : (k + 2) * TILE_ROWS, :], right[:, cols])
            before, block = block, entries(squared)
            if before is not None:
                term = dot(held[:, (k - 1) * TILE_ROWS : k * TILE_ROWS], before)
                total = term if total is None else total + term
        term = dot(held[:, (steps - 1) * TILE_ROWS :], block)
        write(cols, term if total is None else total + term)


def early_kernel(start, sides, table, *refs):
    count = len(sides)
    sources = list(zip(sides, refs[:count], refs[count : 2 * count]))
    target_ref, out_ref, held, left, right = refs[2 * count :]
    column = pl.program_id(0) + start

    @pl.when(table[LIVE, column] == 1)
    def _():
        load_source(table, column, sources, held, left)
        right[...] = target_features(target_ref[0].astype(f32))

        def write(cols, total):
            out_ref[0, :, cols] = total

        near_tile(held, left, right, write)


def source_specs(start, sides, leaf):
    def spec(row, rows):
        return pl.BlockSpec((1, rows, leaf), lambda i, table: (table[row, i + start], 0, 0))

    named = [(PREV, OWN, NEXT)[k] for k in sides]
    return [spec(row, 64) for row in named] + [spec(row, 16) for row in named] + [spec(BOX, 16)]


def tile_scratch(leaf):
    return [pltpu.VMEM((64, leaf), bf16), pltpu.VMEM((leaf, 32), bf16), pltpu.VMEM((32, leaf), bf16)]


def near_early(start, units, table, sides, probes, pairs, own_pair, cost):
    leaf = own_pair.shape[2]
    return pl.pallas_call(
        functools.partial(early_kernel, start, sides),
        grid_spec=pltpu.PrefetchScalarGridSpec(
            num_scalar_prefetch=1,
            grid=(units,),
            in_specs=source_specs(start, sides, leaf),
            out_specs=pl.BlockSpec((1, 64, leaf), lambda i, table: (i, 0, 0)),
            scratch_shapes=tile_scratch(leaf),
        ),
        out_shape=jax.ShapeDtypeStruct((units, 64, leaf), f32),
        compiler_params=params(),
        cost_estimate=cost,
        name="near_early",
    )(table, *probes, *pairs, own_pair)


def last_kernel(sides, table, *refs):
    count = len(sides)
    sources = list(zip(sides, refs[:count], refs[count : 2 * count]))
    target_ref, *early, out_ref, held, left, right = refs[2 * count :]
    column = pl.program_id(0) + LAST_AT
    box = table[BOX, column]

    @pl.when(table[OPENS, column] == 1)
    def _():
        out_ref[...] = jnp.zeros_like(out_ref)
        at = 0
        for ref in early:
            for k in range(ref.shape[0]):

                @pl.when((table[LIVE, at] == 1) & (table[BOX, at] == box))
                def _(ref=ref, k=k):
                    out_ref[0] += ref[k]

                at += 1

    @pl.when(table[LIVE, column] == 1)
    def _():
        load_source(table, column, sources, held, left)
        right[...] = target_features(target_ref[0].astype(f32))

        def write(cols, total):
            out_ref[0, :, cols] += total

        near_tile(held, left, right, write)


def near_last(table, probes, pairs, own_pair, early):
    boxes, _, leaf = own_pair.shape
    sides = (0, 1, 2)
    return pl.pallas_call(
        functools.partial(last_kernel, sides),
        grid_spec=pltpu.PrefetchScalarGridSpec(
            num_scalar_prefetch=1,
            grid=(LAST_UNITS,),
            in_specs=source_specs(LAST_AT, sides, leaf)
            + [pl.BlockSpec(part.shape, lambda i, table: (0, 0, 0), pipeline_mode=pl.Buffered(1)) for part in early],
            out_specs=pl.BlockSpec((1, 64, leaf), lambda i, table: (table[BOX, i + LAST_AT], 0, 0)),
            scratch_shapes=tile_scratch(leaf),
        ),
        out_shape=jax.ShapeDtypeStruct((boxes, 64, leaf), f32),
        compiler_params=params(),
        cost_estimate=SMALL,
        name="near_last",
    )(table, *probes, *pairs, own_pair, *early)


def group_kernel(place_ref, skel_ref, nodes_ref, out_ref):
    nodes, _, rank = nodes_ref.shape
    total = jnp.zeros((64, rank), f32)
    found = jnp.zeros((16, rank), f32)
    skeleton = skel_ref[pl.ds(place_ref[0], 1), :]
    for k in range(nodes):
        total = total + nodes_ref[k, 80:144, :].astype(f32)
        found = found + dot(nodes_ref[k, 64:80, :], one_hot(skeleton, rank, k * rank))
    out_ref[...] = jnp.zeros_like(out_ref)
    out_ref[0:64, :] = total.astype(bf16)
    out_ref[64:80, :] = found.astype(bf16)


def group_pass(place, group_skeleton, nodes):
    rank = nodes.shape[2]
    return pl.pallas_call(
        group_kernel,
        in_specs=[SMEM] + [VMEM] * 2,
        out_specs=VMEM,
        out_shape=jax.ShapeDtypeStruct((GROUP_ROWS, rank), bf16),
        compiler_params=params(),
        name="group_pass",
    )(place, group_skeleton, nodes)


def far_potential(tx_index, ty_index, list_ref, nodes_ref, groups_ref, node_transfer):
    rank = nodes_ref.shape[2]
    target = target_features(groups_ref[tx_index, 64:80, :].astype(f32))
    total = jnp.zeros((64, rank), f32)
    for k in range(groups_ref.shape[0]):
        left = source_features(groups_ref[k, 64:80, :].astype(f32))
        term = dot(groups_ref[k, 0:64, :], entries(dot(left, target)))
        total = total + jnp.where(k != tx_index, term, 0.0)
    group_potential = (total * LN2).astype(bf16)
    target = target_features(nodes_ref[ty_index, 64:80, :].astype(f32))
    total = jnp.zeros((64, rank), f32)
    for k in range(list_ref.shape[1]):
        slot = jnp.clip(list_ref[0, k] - tx_index * nodes_ref.shape[0], 0, nodes_ref.shape[0] - 1)
        left = source_features(nodes_ref[slot, 64:80, :].astype(f32))
        total = total + dot(nodes_ref[slot, 0:64, :], entries(dot(left, target)))
    return (total * LN2 + dot_nt(group_potential, node_transfer)).astype(bf16)


def down_kernel(
    group_at_ref,
    node_at_ref,
    list_ref,
    nodes_ref,
    groups_ref,
    node_transfer_ref,
    transfer_ref,
    down_ref,
    near_ref,
    out_ref,
    potential,
):
    @pl.when(pl.program_id(0) == 0)
    def _():
        potential[...] = far_potential(
            group_at_ref[0], node_at_ref[0], list_ref, nodes_ref, groups_ref, node_transfer_ref[0]
        )

    box_potential = dot_nt(potential[...], transfer_ref[0]).astype(bf16)
    out_ref[0] = (dot(box_potential, down_ref[0]) + near_ref[0] * LN2).astype(bf16)


def down_pass(group_at, node_at, node_list, nodes, groups, node_transfer, box_transfer, down_basis, near):
    boxes, rank, leaf = down_basis.shape

    def whole(shape):
        return pl.BlockSpec(shape, lambda b: (0,) * len(shape))

    def by_box(shape):
        return pl.BlockSpec((1,) + shape, lambda b: (b, 0, 0))

    return pl.pallas_call(
        down_kernel,
        grid=(boxes,),
        in_specs=[
            SMEM,
            SMEM,
            SMEM,
            whole((nodes.shape[0], 80, rank)),
            whole((groups.shape[0], 80, rank)),
            whole((1, rank, rank)),
            by_box((rank, rank)),
            by_box((rank, leaf)),
            by_box((64, leaf)),
        ],
        out_specs=by_box((64, leaf)),
        out_shape=jax.ShapeDtypeStruct((boxes, 64, leaf), bf16),
        scratch_shapes=[pltpu.VMEM((64, rank), bf16)],
        compiler_params=params(),
        name="down_pass",
    )(group_at, node_at, node_list, nodes, groups, node_transfer, box_transfer, down_basis, near)


def shards(
    probes,
    points,
    up_basis,
    down_basis,
    box_skeleton,
    box_transfer,
    node_skeleton,
    node_transfer,
    group_skeleton,
    near_list,
    node_list,
):
    boxes = probes.shape[0]
    n_tx = lax.axis_size("tx")
    n_ty = lax.axis_size("ty")
    tx_index = lax.axis_index("tx")
    ty_index = lax.axis_index("ty")
    node = tx_index * n_ty + ty_index
    base = ((node - 1) * boxes).astype(i32).reshape(1)

    group_at = tx_index.astype(i32).reshape(1)
    node_at = ty_index.astype(i32).reshape(1)
    forward = [(i, i + 1) for i in range(n_ty - 1)]
    backward = [(i + 1, i) for i in range(n_ty - 1)]
    sides = (0, 1, 2)
    all_probes = (lax.ppermute(probes, "ty", forward), probes, lax.ppermute(probes, "ty", backward))
    pair, table, own = prep(
        near_list, base, probes, points, up_basis, box_skeleton, box_transfer, node_skeleton, node_transfer
    )
    all_pairs = (lax.ppermute(pair, "ty", forward), pair, lax.ppermute(pair, "ty", backward))
    nodes = lax.all_gather(own, "ty", axis=0, tiled=False)
    first = near_early(0, OWN_UNITS, table, (1,), (probes,), (pair,), pair, SMALL)
    late_table, first = lax.optimization_barrier((table, first))
    second = near_early(OWN_UNITS, LATE_UNITS, late_table, sides, all_probes, all_pairs, pair, LARGE)
    second, nodes = lax.optimization_barrier((second, nodes))

    group = group_pass(group_at, group_skeleton, nodes)
    third_table, group = lax.optimization_barrier((late_table, group))
    groups = lax.all_gather(group, "tx", axis=0, tiled=False)
    near = near_last(third_table, all_probes, all_pairs, pair, (first, second))
    near, groups = lax.optimization_barrier((near, groups))
    return down_pass(group_at, node_at, node_list, nodes, groups, node_transfer, box_transfer, down_basis, near)


def solution(mesh):
    spec3 = P(("tx", "ty"), None, None)
    spec2 = P(("tx", "ty"), None)
    in_specs = (spec3, spec3, spec3, spec3, spec2, spec3, spec2, spec3, P(), spec2, spec2)
    return jax.shard_map(shards, mesh=mesh, in_specs=in_specs, out_specs=spec3, check_vma=False)
```

```python
import functools
import math

import jax
import jax.numpy as jnp
from jax import lax
from jax.experimental import pallas as pl
from jax.experimental.pallas import tpu as pltpu
from jax.sharding import PartitionSpec as P

bf16 = jnp.bfloat16
f32 = jnp.float32
i32 = jnp.int32

INV_LENGTH = 4.0
LN2 = math.log(2.0)
SCALE = INV_LENGTH / LN2
VMEM = pl.BlockSpec(memory_space=pltpu.VMEM)
SMEM = pl.BlockSpec(memory_space=pltpu.SMEM)
TILE_ROWS = 512
TILE_COLS = 256
OWN_UNITS = 4
LATE_UNITS = 5
GROUP_ROWS = 256
LAST_AT = OWN_UNITS + LATE_UNITS
LAST_UNITS = 8
COLUMNS = LAST_AT + LAST_UNITS
SIDE, BOX, LIVE, OPENS, CLOSES, PREV, OWN, NEXT = range(8)


def params(mib=62):
    return pltpu.CompilerParams(vmem_limit_bytes=mib * 2**20)


SMALL = pl.CostEstimate(flops=1024, bytes_accessed=1024, transcendentals=0)
LARGE = pl.CostEstimate(flops=2**40, bytes_accessed=2**28, transcendentals=0)


def split_points(points):
    scaled = (points - 0.5) * SCALE
    high = scaled.astype(bf16)
    low = (scaled - high.astype(f32)).astype(bf16)
    return high, low


def norm_rows(pair, one_first):
    high = pair[:8]
    low = pair[8:]
    full = high + low
    norm = jnp.sum(full * full, axis=0, keepdims=True)
    first = norm.astype(bf16).astype(f32)
    rest = norm - first
    second = rest.astype(bf16).astype(f32)
    third = rest - second
    row = lax.broadcasted_iota(i32, high.shape, 0)
    base = 3 if one_first else 0
    ones = 0 if one_first else 3
    out = jnp.where((row >= ones) & (row < ones + 3), 1.0, 0.0)
    out = jnp.where(row == base, first, out)
    out = jnp.where(row == base + 1, second, out)
    return jnp.where(row == base + 2, third, out)


def source_features(pair):
    high = pair[:8] * -2.0
    low = pair[8:] * -2.0
    return jnp.concatenate([high, low, high, norm_rows(pair, False)], axis=0).T.astype(bf16)


def target_features(pair):
    high = pair[:8]
    return jnp.concatenate([high, high, pair[8:], norm_rows(pair, True)], axis=0).astype(bf16)


def entries(squared):
    squared = jnp.maximum(squared, 1e-12)
    scaled = squared * lax.rsqrt(squared)
    return (scaled * jnp.exp2(-scaled)).astype(bf16)


def dot(a, b):
    return jnp.dot(a, b, preferred_element_type=f32)


def dot_nt(a, b):
    return lax.dot_general(a, b, (((1,), (1,)), ((), ())), preferred_element_type=f32)


def write_table(near_ref, base_ref, table_ref):
    boxes, width = near_ref.shape
    for column in range(COLUMNS):
        table_ref[SIDE, column] = i32(1)
        table_ref[BOX, column] = i32(boxes - 1)
        for row in (LIVE, OPENS, CLOSES, PREV, OWN, NEXT):
            table_ref[row, column] = i32(0)

    units = []
    for box in range(boxes):
        for entry in range(width):
            named = near_ref[box, entry]
            slot = jnp.clip(named - base_ref[0], 0, 3 * boxes - 1)
            side = (slot >= boxes).astype(i32) + (slot >= 2 * boxes).astype(i32)
            units.append((box, named >= 0, side, slot - side * boxes))

    def put(column, when, box, side, index, hold):
        hold = [jnp.where(when & (side == k), index, hold[k]) for k in range(3)]

        @pl.when(when)
        def _():
            table_ref[SIDE, column] = side
            table_ref[BOX, column] = i32(box)
            table_ref[LIVE, column] = i32(1)
            for k, row in enumerate((PREV, OWN, NEXT)):
                table_ref[row, column] = hold[k]

        return hold

    zero = i32(0)
    own_rank = zero
    rest_rank = zero
    own_count = zero
    for _, live, side, _ in units:
        own_count = own_count + (live & (side == 1)).astype(i32)
    late_limit = jnp.where(own_count >= OWN_UNITS, LATE_UNITS - 2, jnp.where(own_count == OWN_UNITS - 1, LATE_UNITS - 1, LATE_UNITS))
    last_column = i32(LAST_AT)
    own_hold, late_hold, last_hold = [zero] * 3, [zero] * 3, [zero] * 3
    for box in range(boxes):
        opened = last_column
        for _, live, side, index in units[box * width : (box + 1) * width]:
            early = live & (side == 1) & (own_rank < OWN_UNITS)
            own_hold = put(own_rank, early, box, side, index, own_hold)
            own_rank = own_rank + early.astype(i32)
            rest = live & jnp.logical_not(early)
            late = rest & (rest_rank < late_limit)
            late_hold = put(OWN_UNITS + rest_rank, late, box, side, index, late_hold)
            rest_rank = rest_rank + rest.astype(i32)
            last = rest & jnp.logical_not(late)
            last_hold = put(last_column, last, box, side, index, last_hold)
            last_column = last_column + last.astype(i32)
        bare = last_column == opened

        @pl.when(bare)
        def _(column=last_column, box=box, hold=tuple(last_hold)):
            table_ref[BOX, column] = i32(box)
            for k, row in enumerate((PREV, OWN, NEXT)):
                table_ref[row, column] = hold[k]

        last_column = last_column + bare.astype(i32)
        table_ref[OPENS, opened] = i32(1)
        table_ref[CLOSES, last_column - 1] = i32(1)


def one_hot(index_row, size, offset=0):
    rows = lax.broadcasted_iota(i32, (size, index_row.shape[1]), 0) + offset
    return jnp.where(rows == index_row, 1.0, 0.0).astype(bf16)


def prep_kernel(
    near_ref,
    base_ref,
    probes_ref,
    points_ref,
    up_ref,
    box_skel_ref,
    transfer_ref,
    node_skel_ref,
    node_transfer_ref,
    pair_ref,
    table_ref,
    out_ref,
    acc,
    pool,
):
    b = pl.program_id(0)
    boxes = pl.num_programs(0)
    rank = up_ref.shape[1]
    leaf = up_ref.shape[2]

    @pl.when(b == 0)
    def _():
        write_table(near_ref, base_ref, table_ref)
        acc[...] = jnp.zeros_like(acc)

    high, low = split_points(points_ref[0])
    pair = jnp.concatenate([high.astype(f32), low.astype(f32)], axis=0).astype(bf16)
    pair_ref[0] = pair
    weights = dot_nt(probes_ref[0], up_ref[0]).astype(bf16)
    acc[...] += dot(weights, transfer_ref[0])
    pool[b] = dot(pair, one_hot(box_skel_ref[pl.ds(b, 1), :], leaf)).astype(bf16)

    @pl.when(b == boxes - 1)
    def _():
        node_weight = acc[...].astype(bf16)
        out_ref[0:64, :] = node_weight
        found = jnp.zeros((16, rank), f32)
        for k in range(pool.shape[0]):
            found = found + dot(pool[k], one_hot(node_skel_ref[...], rank, k * rank))
        out_ref[64:80, :] = found.astype(bf16)
        out_ref[80:144, :] = dot(node_weight, node_transfer_ref[0]).astype(bf16)


def prep(near_list, base, probes, points, up_basis, box_skeleton, box_transfer, node_skeleton, node_transfer):
    boxes, count, leaf = probes.shape
    rank = up_basis.shape[1]

    def by_box(shape):
        return pl.BlockSpec((1,) + shape, lambda b: (b, 0, 0))

    def whole(shape):
        return pl.BlockSpec(shape, lambda b: (0,) * len(shape))

    return pl.pallas_call(
        prep_kernel,
        grid=(boxes,),
        in_specs=[
            SMEM,
            SMEM,
            by_box((count, leaf)),
            by_box((8, leaf)),
            by_box((rank, leaf)),
            whole((boxes, rank)),
            by_box((rank, rank)),
            whole((1, rank)),
            whole((1, rank, rank)),
        ],
        out_specs=[by_box((16, leaf)), SMEM, whole((144, rank))],
        out_shape=[
            jax.ShapeDtypeStruct((boxes, 16, leaf), bf16),
            jax.ShapeDtypeStruct((8, COLUMNS), i32),
            jax.ShapeDtypeStruct((144, rank), bf16),
        ],
        scratch_shapes=[pltpu.VMEM((64, rank), f32), pltpu.VMEM((boxes, 16, rank), bf16)],
        compiler_params=params(),
        name="prep",
    )(near_list, base, probes, points, up_basis, box_skeleton, box_transfer, node_skeleton, node_transfer)


def load_source(table, column, sources, held, left):
    side = table[SIDE, column]
    for k, probes_ref, pair_ref in sources:

        @pl.when(side == k)
        def _(probes_ref=probes_ref, pair_ref=pair_ref):
            held[...] = probes_ref[0]
            left[...] = source_features(pair_ref[0].astype(f32))


def near_tile(held, left, right, write):
    leaf = left.shape[0]
    steps = leaf // TILE_ROWS
    for j in range(leaf // TILE_COLS):
        cols = slice(j * TILE_COLS, (j + 1) * TILE_COLS)
        total = None
        block = None
        ahead = dot(left[0:TILE_ROWS, :], right[:, cols])
        for k in range(steps):
            squared = ahead
            if k + 1 < steps:
                ahead = dot(left[(k + 1) * TILE_ROWS : (k + 2) * TILE_ROWS, :], right[:, cols])
            before, block = block, entries(squared)
            if before is not None:
                term = dot(held[:, (k - 1) * TILE_ROWS : k * TILE_ROWS], before)
                total = term if total is None else total + term
        term = dot(held[:, (steps - 1) * TILE_ROWS :], block)
        write(cols, term if total is None else total + term)


def early_kernel(start, sides, table, *refs):
    count = len(sides)
    sources = list(zip(sides, refs[:count], refs[count : 2 * count]))
    target_ref, out_ref, held, left, right = refs[2 * count :]
    column = pl.program_id(0) + start

    @pl.when(table[LIVE, column] == 1)
    def _():
        load_source(table, column, sources, held, left)
        right[...] = target_features(target_ref[0].astype(f32))

        def write(cols, total):
            out_ref[0, :, cols] = total

        near_tile(held, left, right, write)


def source_specs(start, sides, leaf):
    def spec(row, rows):
        return pl.BlockSpec((1, rows, leaf), lambda i, table: (table[row, i + start], 0, 0))

    named = [(PREV, OWN, NEXT)[k] for k in sides]
    return [spec(row, 64) for row in named] + [spec(row, 16) for row in named] + [spec(BOX, 16)]


def tile_scratch(leaf):
    return [pltpu.VMEM((64, leaf), bf16), pltpu.VMEM((leaf, 32), bf16), pltpu.VMEM((32, leaf), bf16)]


def near_early(start, units, table, sides, probes, pairs, own_pair, cost):
    leaf = own_pair.shape[2]
    return pl.pallas_call(
        functools.partial(early_kernel, start, sides),
        grid_spec=pltpu.PrefetchScalarGridSpec(
            num_scalar_prefetch=1,
            grid=(units,),
            in_specs=source_specs(start, sides, leaf),
            out_specs=pl.BlockSpec((1, 64, leaf), lambda i, table: (i, 0, 0)),
            scratch_shapes=tile_scratch(leaf),
        ),
        out_shape=jax.ShapeDtypeStruct((units, 64, leaf), f32),
        compiler_params=params(),
        cost_estimate=cost,
        name="near_early",
    )(table, *probes, *pairs, own_pair)


def last_kernel(sides, table, *refs):
    count = len(sides)
    sources = list(zip(sides, refs[:count], refs[count : 2 * count]))
    target_ref, *early, out_ref, held, left, right = refs[2 * count :]
    column = pl.program_id(0) + LAST_AT
    box = table[BOX, column]

    @pl.when(table[OPENS, column] == 1)
    def _():
        out_ref[...] = jnp.zeros_like(out_ref)
        at = 0
        for ref in early:
            for k in range(ref.shape[0]):

                @pl.when((table[LIVE, at] == 1) & (table[BOX, at] == box))
                def _(ref=ref, k=k):
                    out_ref[0] += ref[k]

                at += 1

    @pl.when(table[LIVE, column] == 1)
    def _():
        load_source(table, column, sources, held, left)
        right[...] = target_features(target_ref[0].astype(f32))

        def write(cols, total):
            out_ref[0, :, cols] += total

        near_tile(held, left, right, write)


def near_last(table, probes, pairs, own_pair, early):
    boxes, _, leaf = own_pair.shape
    sides = (0, 1, 2)
    return pl.pallas_call(
        functools.partial(last_kernel, sides),
        grid_spec=pltpu.PrefetchScalarGridSpec(
            num_scalar_prefetch=1,
            grid=(LAST_UNITS,),
            in_specs=source_specs(LAST_AT, sides, leaf)
            + [pl.BlockSpec(part.shape, lambda i, table: (0, 0, 0), pipeline_mode=pl.Buffered(1)) for part in early],
            out_specs=pl.BlockSpec((1, 64, leaf), lambda i, table: (table[BOX, i + LAST_AT], 0, 0)),
            scratch_shapes=tile_scratch(leaf),
        ),
        out_shape=jax.ShapeDtypeStruct((boxes, 64, leaf), f32),
        compiler_params=params(),
        cost_estimate=SMALL,
        name="near_last",
    )(table, *probes, *pairs, own_pair, *early)


def group_kernel(place_ref, skel_ref, nodes_ref, out_ref):
    nodes, _, rank = nodes_ref.shape
    total = jnp.zeros((64, rank), f32)
    found = jnp.zeros((16, rank), f32)
    skeleton = skel_ref[pl.ds(place_ref[0], 1), :]
    for k in range(nodes):
        total = total + nodes_ref[k, 80:144, :].astype(f32)
        found = found + dot(nodes_ref[k, 64:80, :], one_hot(skeleton, rank, k * rank))
    out_ref[...] = jnp.zeros_like(out_ref)
    out_ref[0:64, :] = total.astype(bf16)
    out_ref[64:80, :] = found.astype(bf16)


def group_pass(place, group_skeleton, nodes):
    rank = nodes.shape[2]
    return pl.pallas_call(
        group_kernel,
        in_specs=[SMEM] + [VMEM] * 2,
        out_specs=VMEM,
        out_shape=jax.ShapeDtypeStruct((GROUP_ROWS, rank), bf16),
        compiler_params=params(),
        name="group_pass",
    )(place, group_skeleton, nodes)


def far_potential(tx_index, ty_index, list_ref, nodes_ref, groups_ref, node_transfer):
    rank = nodes_ref.shape[2]
    target = target_features(groups_ref[tx_index, 64:80, :].astype(f32))
    total = jnp.zeros((64, rank), f32)
    for k in range(groups_ref.shape[0]):
        left = source_features(groups_ref[k, 64:80, :].astype(f32))
        term = dot(groups_ref[k, 0:64, :], entries(dot(left, target)))
        total = total + jnp.where(k != tx_index, term, 0.0)
    group_potential = (total * LN2).astype(bf16)
    target = target_features(nodes_ref[ty_index, 64:80, :].astype(f32))
    total = jnp.zeros((64, rank), f32)
    for k in range(list_ref.shape[1]):
        slot = jnp.clip(list_ref[0, k] - tx_index * nodes_ref.shape[0], 0, nodes_ref.shape[0] - 1)
        left = source_features(nodes_ref[slot, 64:80, :].astype(f32))
        total = total + dot(nodes_ref[slot, 0:64, :], entries(dot(left, target)))
    return (total * LN2 + dot_nt(group_potential, node_transfer)).astype(bf16)


def down_kernel(
    group_at_ref,
    node_at_ref,
    list_ref,
    nodes_ref,
    groups_ref,
    node_transfer_ref,
    transfer_ref,
    down_ref,
    near_ref,
    out_ref,
    potential,
):
    @pl.when(pl.program_id(0) == 0)
    def _():
        potential[...] = far_potential(
            group_at_ref[0], node_at_ref[0], list_ref, nodes_ref, groups_ref, node_transfer_ref[0]
        )

    box_potential = dot_nt(potential[...], transfer_ref[0]).astype(bf16)
    out_ref[0] = (dot(box_potential, down_ref[0]) + near_ref[0] * LN2).astype(bf16)


def down_pass(group_at, node_at, node_list, nodes, groups, node_transfer, box_transfer, down_basis, near):
    boxes, rank, leaf = down_basis.shape

    def whole(shape):
        return pl.BlockSpec(shape, lambda b: (0,) * len(shape))

    def by_box(shape):
        return pl.BlockSpec((1,) + shape, lambda b: (b, 0, 0))

    return pl.pallas_call(
        down_kernel,
        grid=(boxes,),
        in_specs=[
            SMEM,
            SMEM,
            SMEM,
            whole((nodes.shape[0], 80, rank)),
            whole((groups.shape[0], 80, rank)),
            whole((1, rank, rank)),
            by_box((rank, rank)),
            by_box((rank, leaf)),
            by_box((64, leaf)),
        ],
        out_specs=by_box((64, leaf)),
        out_shape=jax.ShapeDtypeStruct((boxes, 64, leaf), bf16),
        scratch_shapes=[pltpu.VMEM((64, rank), bf16)],
        compiler_params=params(),
        name="down_pass",
    )(group_at, node_at, node_list, nodes, groups, node_transfer, box_transfer, down_basis, near)


def shards(
    probes,
    points,
    up_basis,
    down_basis,
    box_skeleton,
    box_transfer,
    node_skeleton,
    node_transfer,
    group_skeleton,
    near_list,
    node_list,
):
    boxes = probes.shape[0]
    n_tx = lax.axis_size("tx")
    n_ty = lax.axis_size("ty")
    tx_index = lax.axis_index("tx")
    ty_index = lax.axis_index("ty")
    node = tx_index * n_ty + ty_index
    base = ((node - 1) * boxes).astype(i32).reshape(1)

    group_at = tx_index.astype(i32).reshape(1)
    node_at = ty_index.astype(i32).reshape(1)
    forward = [(i, i + 1) for i in range(n_ty - 1)]
    backward = [(i + 1, i) for i in range(n_ty - 1)]
    sides = (0, 1, 2)
    all_probes = (lax.ppermute(probes, "ty", forward), probes, lax.ppermute(probes, "ty", backward))
    pair, table, own = prep(
        near_list, base, probes, points, up_basis, box_skeleton, box_transfer, node_skeleton, node_transfer
    )
    all_pairs = (lax.ppermute(pair, "ty", forward), pair, lax.ppermute(pair, "ty", backward))
    nodes = lax.all_gather(own, "ty", axis=0, tiled=False)
    first = near_early(0, OWN_UNITS, table, (1,), (probes,), (pair,), pair, SMALL)
    late_table, first = lax.optimization_barrier((table, first))
    second = near_early(OWN_UNITS, LATE_UNITS, late_table, sides, all_probes, all_pairs, pair, LARGE)
    second, nodes = lax.optimization_barrier((second, nodes))

    group = group_pass(group_at, group_skeleton, nodes)
    third_table, group = lax.optimization_barrier((late_table, group))
    groups = lax.all_gather(group, "tx", axis=0, tiled=False)
    near = near_last(third_table, all_probes, all_pairs, pair, (first, second))
    near, groups = lax.optimization_barrier((near, groups))
    return down_pass(group_at, node_at, node_list, nodes, groups, node_transfer, box_transfer, down_basis, near)


def solution(mesh):
    spec3 = P(("tx", "ty"), None, None)
    spec2 = P(("tx", "ty"), None)
    in_specs = (spec3, spec3, spec3, spec3, spec2, spec3, spec2, spec3, P(), spec2, spec2)
    return jax.shard_map(shards, mesh=mesh, in_specs=in_specs, out_specs=spec3, check_vma=False)
```

```python
import functools
import math

import jax
import jax.numpy as jnp
from jax import lax
from jax.experimental import pallas as pl
from jax.experimental.pallas import tpu as pltpu
from jax.sharding import PartitionSpec as P

bf16 = jnp.bfloat16
f32 = jnp.float32
i32 = jnp.int32

INV_LENGTH = 4.0
LN2 = math.log(2.0)
SCALE = INV_LENGTH / LN2
VMEM = pl.BlockSpec(memory_space=pltpu.VMEM)
SMEM = pl.BlockSpec(memory_space=pltpu.SMEM)
TILE_ROWS = 512
TILE_COLS = 256
OWN_UNITS = 4
LATE_UNITS = 5
GROUP_ROWS = 256
LAST_AT = OWN_UNITS + LATE_UNITS
LAST_UNITS = 8
COLUMNS = LAST_AT + LAST_UNITS
SIDE, BOX, LIVE, OPENS, CLOSES, PREV, OWN, NEXT = range(8)


def params(mib=62):
    return pltpu.CompilerParams(vmem_limit_bytes=mib * 2**20)


SMALL = pl.CostEstimate(flops=1024, bytes_accessed=1024, transcendentals=0)
LARGE = pl.CostEstimate(flops=2**40, bytes_accessed=2**28, transcendentals=0)


def split_points(points):
    scaled = (points - 0.5) * SCALE
    high = scaled.astype(bf16)
    low = (scaled - high.astype(f32)).astype(bf16)
    return high, low


def norm_rows(pair, one_first):
    high = pair[:8]
    low = pair[8:]
    full = high + low
    norm = jnp.sum(full * full, axis=0, keepdims=True)
    first = norm.astype(bf16).astype(f32)
    rest = norm - first
    second = rest.astype(bf16).astype(f32)
    third = rest - second
    row = lax.broadcasted_iota(i32, high.shape, 0)
    base = 3 if one_first else 0
    ones = 0 if one_first else 3
    out = jnp.where((row >= ones) & (row < ones + 3), 1.0, 0.0)
    out = jnp.where(row == base, first, out)
    out = jnp.where(row == base + 1, second, out)
    return jnp.where(row == base + 2, third, out)


def source_features(pair):
    high = pair[:8] * -2.0
    low = pair[8:] * -2.0
    return jnp.concatenate([high, low, high, norm_rows(pair, False)], axis=0).T.astype(bf16)


def target_features(pair):
    high = pair[:8]
    return jnp.concatenate([high, high, pair[8:], norm_rows(pair, True)], axis=0).astype(bf16)


def entries(squared):
    squared = jnp.maximum(squared, 1e-12)
    scaled = squared * lax.rsqrt(squared)
    return (scaled * jnp.exp2(-scaled)).astype(bf16)


def dot(a, b):
    return jnp.dot(a, b, preferred_element_type=f32)


def dot_nt(a, b):
    return lax.dot_general(a, b, (((1,), (1,)), ((), ())), preferred_element_type=f32)


def write_table(near_ref, base_ref, table_ref):
    boxes, width = near_ref.shape
    for column in range(COLUMNS):
        table_ref[SIDE, column] = i32(1)
        table_ref[BOX, column] = i32(boxes - 1)
        for row in (LIVE, OPENS, CLOSES, PREV, OWN, NEXT):
            table_ref[row, column] = i32(0)

    units = []
    for box in range(boxes):
        for entry in range(width):
            named = near_ref[box, entry]
            slot = jnp.clip(named - base_ref[0], 0, 3 * boxes - 1)
            side = (slot >= boxes).astype(i32) + (slot >= 2 * boxes).astype(i32)
            units.append((box, named >= 0, side, slot - side * boxes))

    def put(column, when, box, side, index, hold):
        hold = [jnp.where(when & (side == k), index, hold[k]) for k in range(3)]

        @pl.when(when)
        def _():
            table_ref[SIDE, column] = side
            table_ref[BOX, column] = i32(box)
            table_ref[LIVE, column] = i32(1)
            for k, row in enumerate((PREV, OWN, NEXT)):
                table_ref[row, column] = hold[k]

        return hold

    zero = i32(0)
    own_rank = zero
    rest_rank = zero
    own_count = zero
    count = zero
    for _, live, side, _ in units:
        own_count = own_count + (live & (side == 1)).astype(i32)
        count = count + live.astype(i32)
    many = jnp.where(count == boxes * width, LATE_UNITS - 1, LATE_UNITS - 2)
    some = jnp.where(count >= boxes * width - 1, LATE_UNITS, LATE_UNITS - 1)
    late_limit = jnp.where(own_count >= OWN_UNITS, many, jnp.where(own_count == OWN_UNITS - 1, some, LATE_UNITS))
    last_column = i32(LAST_AT)
    own_hold, late_hold, last_hold = [zero] * 3, [zero] * 3, [zero] * 3
    for box in range(boxes):
        opened = last_column
        for _, live, side, index in units[box * width : (box + 1) * width]:
            early = live & (side == 1) & (own_rank < OWN_UNITS)
            own_hold = put(own_rank, early, box, side, index, own_hold)
            own_rank = own_rank + early.astype(i32)
            rest = live & jnp.logical_not(early)
            late = rest & (rest_rank < late_limit)
            late_hold = put(OWN_UNITS + rest_rank, late, box, side, index, late_hold)
            rest_rank = rest_rank + rest.astype(i32)
            last = rest & jnp.logical_not(late)
            last_hold = put(last_column, last, box, side, index, last_hold)
            last_column = last_column + last.astype(i32)
        bare = last_column == opened

        @pl.when(bare)
        def _(column=last_column, box=box, hold=tuple(last_hold)):
            table_ref[BOX, column] = i32(box)
            for k, row in enumerate((PREV, OWN, NEXT)):
                table_ref[row, column] = hold[k]

        last_column = last_column + bare.astype(i32)
        table_ref[OPENS, opened] = i32(1)
        table_ref[CLOSES, last_column - 1] = i32(1)


def one_hot(index_row, size, offset=0):
    rows = lax.broadcasted_iota(i32, (size, index_row.shape[1]), 0) + offset
    return jnp.where(rows == index_row, 1.0, 0.0).astype(bf16)


def prep_kernel(
    near_ref,
    base_ref,
    probes_ref,
    points_ref,
    up_ref,
    box_skel_ref,
    transfer_ref,
    node_skel_ref,
    node_transfer_ref,
    pair_ref,
    table_ref,
    out_ref,
    acc,
    pool,
):
    b = pl.program_id(0)
    boxes = pl.num_programs(0)
    rank = up_ref.shape[1]
    leaf = up_ref.shape[2]

    @pl.when(b == 0)
    def _():
        write_table(near_ref, base_ref, table_ref)
        acc[...] = jnp.zeros_like(acc)

    high, low = split_points(points_ref[0])
    pair = jnp.concatenate([high.astype(f32), low.astype(f32)], axis=0).astype(bf16)
    pair_ref[0] = pair
    weights = dot_nt(probes_ref[0], up_ref[0]).astype(bf16)
    acc[...] += dot(weights, transfer_ref[0])
    pool[b] = dot(pair, one_hot(box_skel_ref[pl.ds(b, 1), :], leaf)).astype(bf16)

    @pl.when(b == boxes - 1)
    def _():
        node_weight = acc[...].astype(bf16)
        out_ref[0:64, :] = node_weight
        found = jnp.zeros((16, rank), f32)
        for k in range(pool.shape[0]):
            found = found + dot(pool[k], one_hot(node_skel_ref[...], rank, k * rank))
        out_ref[64:80, :] = found.astype(bf16)
        out_ref[80:144, :] = dot(node_weight, node_transfer_ref[0]).astype(bf16)


def prep(near_list, base, probes, points, up_basis, box_skeleton, box_transfer, node_skeleton, node_transfer):
    boxes, count, leaf = probes.shape
    rank = up_basis.shape[1]

    def by_box(shape):
        return pl.BlockSpec((1,) + shape, lambda b: (b, 0, 0))

    def whole(shape):
        return pl.BlockSpec(shape, lambda b: (0,) * len(shape))

    return pl.pallas_call(
        prep_kernel,
        grid=(boxes,),
        in_specs=[
            SMEM,
            SMEM,
            by_box((count, leaf)),
            by_box((8, leaf)),
            by_box((rank, leaf)),
            whole((boxes, rank)),
            by_box((rank, rank)),
            whole((1, rank)),
            whole((1, rank, rank)),
        ],
        out_specs=[by_box((16, leaf)), SMEM, whole((144, rank))],
        out_shape=[
            jax.ShapeDtypeStruct((boxes, 16, leaf), bf16),
            jax.ShapeDtypeStruct((8, COLUMNS), i32),
            jax.ShapeDtypeStruct((144, rank), bf16),
        ],
        scratch_shapes=[pltpu.VMEM((64, rank), f32), pltpu.VMEM((boxes, 16, rank), bf16)],
        compiler_params=params(),
        name="prep",
    )(near_list, base, probes, points, up_basis, box_skeleton, box_transfer, node_skeleton, node_transfer)


def load_source(table, column, sources, held, left):
    side = table[SIDE, column]
    for k, probes_ref, pair_ref in sources:

        @pl.when(side == k)
        def _(probes_ref=probes_ref, pair_ref=pair_ref):
            held[...] = probes_ref[0]
            left[...] = source_features(pair_ref[0].astype(f32))


def near_tile(held, left, right, write):
    leaf = left.shape[0]
    steps = leaf // TILE_ROWS
    for j in range(leaf // TILE_COLS):
        cols = slice(j * TILE_COLS, (j + 1) * TILE_COLS)
        total = None
        block = None
        ahead = dot(left[0:TILE_ROWS, :], right[:, cols])
        for k in range(steps):
            squared = ahead
            if k + 1 < steps:
                ahead = dot(left[(k + 1) * TILE_ROWS : (k + 2) * TILE_ROWS, :], right[:, cols])
            before, block = block, entries(squared)
            if before is not None:
                term = dot(held[:, (k - 1) * TILE_ROWS : k * TILE_ROWS], before)
                total = term if total is None else total + term
        term = dot(held[:, (steps - 1) * TILE_ROWS :], block)
        write(cols, term if total is None else total + term)


def early_kernel(start, sides, table, *refs):
    count = len(sides)
    sources = list(zip(sides, refs[:count], refs[count : 2 * count]))
    target_ref, out_ref, held, left, right = refs[2 * count :]
    column = pl.program_id(0) + start

    @pl.when(table[LIVE, column] == 1)
    def _():
        load_source(table, column, sources, held, left)
        right[...] = target_features(target_ref[0].astype(f32))

        def write(cols, total):
            out_ref[0, :, cols] = total

        near_tile(held, left, right, write)


def source_specs(start, sides, leaf):
    def spec(row, rows):
        return pl.BlockSpec((1, rows, leaf), lambda i, table: (table[row, i + start], 0, 0))

    named = [(PREV, OWN, NEXT)[k] for k in sides]
    return [spec(row, 64) for row in named] + [spec(row, 16) for row in named] + [spec(BOX, 16)]


def tile_scratch(leaf):
    return [pltpu.VMEM((64, leaf), bf16), pltpu.VMEM((leaf, 32), bf16), pltpu.VMEM((32, leaf), bf16)]


def near_early(start, units, table, sides, probes, pairs, own_pair, cost):
    leaf = own_pair.shape[2]
    return pl.pallas_call(
        functools.partial(early_kernel, start, sides),
        grid_spec=pltpu.PrefetchScalarGridSpec(
            num_scalar_prefetch=1,
            grid=(units,),
            in_specs=source_specs(start, sides, leaf),
            out_specs=pl.BlockSpec((1, 64, leaf), lambda i, table: (i, 0, 0)),
            scratch_shapes=tile_scratch(leaf),
        ),
        out_shape=jax.ShapeDtypeStruct((units, 64, leaf), f32),
        compiler_params=params(),
        cost_estimate=cost,
        name="near_early",
    )(table, *probes, *pairs, own_pair)


def last_kernel(sides, table, *refs):
    count = len(sides)
    sources = list(zip(sides, refs[:count], refs[count : 2 * count]))
    target_ref, *early, out_ref, held, left, right = refs[2 * count :]
    column = pl.program_id(0) + LAST_AT
    box = table[BOX, column]

    @pl.when(table[OPENS, column] == 1)
    def _():
        out_ref[...] = jnp.zeros_like(out_ref)
        at = 0
        for ref in early:
            for k in range(ref.shape[0]):

                @pl.when((table[LIVE, at] == 1) & (table[BOX, at] == box))
                def _(ref=ref, k=k):
                    out_ref[0] += ref[k]

                at += 1

    @pl.when(table[LIVE, column] == 1)
    def _():
        load_source(table, column, sources, held, left)
        right[...] = target_features(target_ref[0].astype(f32))

        def write(cols, total):
            out_ref[0, :, cols] += total

        near_tile(held, left, right, write)


def near_last(table, probes, pairs, own_pair, early):
    boxes, _, leaf = own_pair.shape
    sides = (0, 1, 2)
    return pl.pallas_call(
        functools.partial(last_kernel, sides),
        grid_spec=pltpu.PrefetchScalarGridSpec(
            num_scalar_prefetch=1,
            grid=(LAST_UNITS,),
            in_specs=source_specs(LAST_AT, sides, leaf)
            + [pl.BlockSpec(part.shape, lambda i, table: (0, 0, 0), pipeline_mode=pl.Buffered(1)) for part in early],
            out_specs=pl.BlockSpec((1, 64, leaf), lambda i, table: (table[BOX, i + LAST_AT], 0, 0)),
            scratch_shapes=tile_scratch(leaf),
        ),
        out_shape=jax.ShapeDtypeStruct((boxes, 64, leaf), f32),
        compiler_params=params(),
        cost_estimate=SMALL,
        name="near_last",
    )(table, *probes, *pairs, own_pair, *early)


def group_kernel(place_ref, skel_ref, nodes_ref, out_ref):
    nodes, _, rank = nodes_ref.shape
    total = jnp.zeros((64, rank), f32)
    found = jnp.zeros((16, rank), f32)
    skeleton = skel_ref[pl.ds(place_ref[0], 1), :]
    for k in range(nodes):
        total = total + nodes_ref[k, 80:144, :].astype(f32)
        found = found + dot(nodes_ref[k, 64:80, :], one_hot(skeleton, rank, k * rank))
    out_ref[...] = jnp.zeros_like(out_ref)
    out_ref[0:64, :] = total.astype(bf16)
    out_ref[64:80, :] = found.astype(bf16)


def group_pass(place, group_skeleton, nodes):
    rank = nodes.shape[2]
    return pl.pallas_call(
        group_kernel,
        in_specs=[SMEM] + [VMEM] * 2,
        out_specs=VMEM,
        out_shape=jax.ShapeDtypeStruct((GROUP_ROWS, rank), bf16),
        compiler_params=params(),
        name="group_pass",
    )(place, group_skeleton, nodes)


def far_potential(tx_index, ty_index, list_ref, nodes_ref, groups_ref, node_transfer):
    rank = nodes_ref.shape[2]
    target = target_features(groups_ref[tx_index, 64:80, :].astype(f32))
    total = jnp.zeros((64, rank), f32)
    for k in range(groups_ref.shape[0]):
        left = source_features(groups_ref[k, 64:80, :].astype(f32))
        term = dot(groups_ref[k, 0:64, :], entries(dot(left, target)))
        total = total + jnp.where(k != tx_index, term, 0.0)
    group_potential = (total * LN2).astype(bf16)
    target = target_features(nodes_ref[ty_index, 64:80, :].astype(f32))
    total = jnp.zeros((64, rank), f32)
    for k in range(list_ref.shape[1]):
        slot = jnp.clip(list_ref[0, k] - tx_index * nodes_ref.shape[0], 0, nodes_ref.shape[0] - 1)
        left = source_features(nodes_ref[slot, 64:80, :].astype(f32))
        total = total + dot(nodes_ref[slot, 0:64, :], entries(dot(left, target)))
    return (total * LN2 + dot_nt(group_potential, node_transfer)).astype(bf16)


def down_kernel(
    group_at_ref,
    node_at_ref,
    list_ref,
    nodes_ref,
    groups_ref,
    node_transfer_ref,
    transfer_ref,
    down_ref,
    near_ref,
    out_ref,
    potential,
):
    @pl.when(pl.program_id(0) == 0)
    def _():
        potential[...] = far_potential(
            group_at_ref[0], node_at_ref[0], list_ref, nodes_ref, groups_ref, node_transfer_ref[0]
        )

    for k in range(out_ref.shape[0]):
        box_potential = dot_nt(potential[...], transfer_ref[k]).astype(bf16)
        out_ref[k] = (dot(box_potential, down_ref[k]) + near_ref[k] * LN2).astype(bf16)


def down_pass(group_at, node_at, node_list, nodes, groups, node_transfer, box_transfer, down_basis, near):
    boxes, rank, leaf = down_basis.shape

    def whole(shape):
        return pl.BlockSpec(shape, lambda b: (0,) * len(shape))

    def by_box(shape):
        return pl.BlockSpec((boxes // 2,) + shape, lambda b: (b, 0, 0))

    return pl.pallas_call(
        down_kernel,
        grid=(2,),
        in_specs=[
            SMEM,
            SMEM,
            SMEM,
            whole((nodes.shape[0], 80, rank)),
            whole((groups.shape[0], 80, rank)),
            whole((1, rank, rank)),
            by_box((rank, rank)),
            by_box((rank, leaf)),
            by_box((64, leaf)),
        ],
        out_specs=by_box((64, leaf)),
        out_shape=jax.ShapeDtypeStruct((boxes, 64, leaf), bf16),
        scratch_shapes=[pltpu.VMEM((64, rank), bf16)],
        compiler_params=params(),
        name="down_pass",
    )(group_at, node_at, node_list, nodes, groups, node_transfer, box_transfer, down_basis, near)


def shards(
    probes,
    points,
    up_basis,
    down_basis,
    box_skeleton,
    box_transfer,
    node_skeleton,
    node_transfer,
    group_skeleton,
    near_list,
    node_list,
):
    boxes = probes.shape[0]
    n_tx = lax.axis_size("tx")
    n_ty = lax.axis_size("ty")
    tx_index = lax.axis_index("tx")
    ty_index = lax.axis_index("ty")
    node = tx_index * n_ty + ty_index
    base = ((node - 1) * boxes).astype(i32).reshape(1)

    group_at = tx_index.astype(i32).reshape(1)
    node_at = ty_index.astype(i32).reshape(1)
    forward = [(i, i + 1) for i in range(n_ty - 1)]
    backward = [(i + 1, i) for i in range(n_ty - 1)]
    sides = (0, 1, 2)
    all_probes = (lax.ppermute(probes, "ty", forward), probes, lax.ppermute(probes, "ty", backward))
    pair, table, own = prep(
        near_list, base, probes, points, up_basis, box_skeleton, box_transfer, node_skeleton, node_transfer
    )
    all_pairs = (lax.ppermute(pair, "ty", forward), pair, lax.ppermute(pair, "ty", backward))
    nodes = lax.all_gather(own, "ty", axis=0, tiled=False)
    first = near_early(0, OWN_UNITS, table, (1,), (probes,), (pair,), pair, SMALL)
    late_table, first = lax.optimization_barrier((table, first))
    second = near_early(OWN_UNITS, LATE_UNITS, late_table, sides, all_probes, all_pairs, pair, LARGE)
    second, nodes = lax.optimization_barrier((second, nodes))

    group = group_pass(group_at, group_skeleton, nodes)
    third_table, group = lax.optimization_barrier((late_table, group))
    groups = lax.all_gather(group, "tx", axis=0, tiled=False)
    near = near_last(third_table, all_probes, all_pairs, pair, (first, second))
    near, groups = lax.optimization_barrier((near, groups))
    return down_pass(group_at, node_at, node_list, nodes, groups, node_transfer, box_transfer, down_basis, near)


def solution(mesh):
    spec3 = P(("tx", "ty"), None, None)
    spec2 = P(("tx", "ty"), None)
    in_specs = (spec3, spec3, spec3, spec3, spec2, spec3, spec2, spec3, P(), spec2, spec2)
    return jax.shard_map(shards, mesh=mesh, in_specs=in_specs, out_specs=spec3, check_vma=False)
```
